256 devices in a mesh: context: 32 (over y, x, core), head: 8 (over z).
Axes of the slice: x: 4, y: 4, z: 8, core: 2. Of those that a mesh axis runs over, the one named last changes fastest.
Arguments:
- queries: bfloat16 [4096, 64, 128], P('context', 'head'), may hold values from -200 to 200
- keys: bfloat16 [4096, 8, 128], P('context', 'head'), may hold values from -6 to 6
- c_proj: bfloat16 [4096, 64, 128], P('context', 'head'), may hold values from -0.3125 to 0.3125
- b_proj: bfloat16 [4096, 8, 128], P('context', 'head'), may hold values from -0.3125 to 0.3125
- log_decay: float32 [4096, 64], P('context', 'head'), may hold values from -0.6 to 0, as said below
Outputs:
- distill_loss: float32 [], replicated
- grad_c: float32 [4096, 64, 128], P('context', 'head')
- grad_b: float32 [4096, 8, 128], P('context', 'head')
The draws below stay inside these ranges and needn't reach their ends.
Inputs may be any that keep to these rules, and one draw needn't show every extreme that they name: `log_decay`: negative.
All inputs are finite; a program needn't handle non-finite values.
Results may differ from the reference program's by a relative error of at most 0.00076.
Values may be sent and summed in bfloat16 or wider, within the bound.
No kernel may reach another device: no remote copies, remote signals or barrier semaphores. Data moves between devices by JAX's collectives and lax.ppermute only.
A program may use at most 128 MiB of HBM per device.

```python
import math
import jax
import jax.numpy as jnp
from jax import lax

HEAD_COUNT = 64
KV_HEADS = 8
HD = 128
TOKEN_LENGTH = 4096


def shared_keys(seed_key):
    return jnp.clip(jax.random.normal(seed_key, (TOKEN_LENGTH, KV_HEADS, HD), jnp.float32), -6.0, 6.0)


def draw_keys(key, part):
    return shared_keys(key).astype(jnp.bfloat16)


def draw_queries(key, part):
    key = jax.random.fold_in(key, 7)
    seed_a = jax.random.fold_in(key, 0)
    drawn_rows = jnp.clip(jax.random.normal(seed_a, (TOKEN_LENGTH, HEAD_COUNT, HD), jnp.float32), -6.0, 6.0)
    return drawn_rows.astype(jnp.bfloat16)


def draw_log_decay(key, part):
    key = jax.random.fold_in(key, 11)
    seed_a, seed_b, seed_c, seed_d, random_seed_fifth, random_seed_sixth = jax.random.split(key, 6)
    slow_share = 0.5
    slow_heads = jax.random.uniform(seed_a, (1, HEAD_COUNT), jnp.float32) < slow_share
    keep_share = jax.random.uniform(seed_b, (1, HEAD_COUNT), jnp.float32, 0.4, 0.8)
    slow_rate = -jnp.log(keep_share) / TOKEN_LENGTH
    fast_rate = 1.0 / jax.random.uniform(seed_c, (1, HEAD_COUNT), jnp.float32, 30.0, 50.0)
    baseline_rate = jnp.where(slow_heads, slow_rate, fast_rate)
    jitter_level = jnp.exp(jax.random.uniform(seed_d, (TOKEN_LENGTH, HEAD_COUNT), jnp.float32, math.log(0.7), math.log(1.4)))
    spike_events = jax.random.randint(random_seed_fifth, (2,), 0, TOKEN_LENGTH)
    spike_rows = jnp.any(jnp.arange(TOKEN_LENGTH, dtype=jnp.int32)[:, None] == spike_events[None, :], axis=1)[:, None]
    spike_loss = jnp.log(jax.random.uniform(random_seed_sixth, (1, HEAD_COUNT), jnp.float32, 0.6, 0.8))
    return -baseline_rate * jitter_level + jnp.where(spike_rows, spike_loss, 0.0)


def levels(stream_key, shape, shards, smallest, high):
    loudness = 1.0
    for dim, shards_of in shards:
        steps = jax.random.uniform(jax.random.fold_in(jax.random.fold_in(stream_key, 6), dim), (shards_of,), jnp.float32, smallest / len(shards), high / len(shards))
        loudness = loudness * jnp.repeat(jnp.exp(steps), shape[dim] // shards_of).reshape((-1,) + (1,) * (len(shape) - 1 - dim))
    return loudness


def noise(own_key, dims, width, reach, shards=(), kind=jnp.bfloat16):
    result = width * jax.random.normal(own_key, dims, jnp.float32)
    if shards:
        result = result * levels(own_key, dims, shards, -0.22, 0.18)
    return jnp.clip(result, -reach, reach).astype(kind)


def setup_inputs(seed: int = 0) -> dict:
    arg_keys = jax.random.split(jax.random.key(seed), 6)
    return {
        "queries": draw_queries(jax.random.fold_in(arg_keys[5], 71), 0),
        "keys": draw_keys(jax.random.fold_in(arg_keys[5], 71), 0),
        "c_proj": noise(arg_keys[2], (TOKEN_LENGTH, HEAD_COUNT, HD), 0.05, 0.3125, ((0, 32), (1, 8))),
        "b_proj": noise(arg_keys[3], (TOKEN_LENGTH, KV_HEADS, HD), 0.05, 0.3125, ((0, 32), (1, 8))),
        "log_decay": draw_log_decay(jax.random.fold_in(arg_keys[5], 71), 0),
    }


def head_terms(query_rows, key_rows, c_rows, b_rows, cum_rows):
    length = query_rows.shape[0]
    positions = jnp.arange(length, dtype=jnp.int32)
    causal = positions[:, None] >= positions[None, :]
    scale_factor = 1.0 / math.sqrt(query_rows.shape[1])
    scores = jnp.dot(query_rows, key_rows.T, precision=lax.Precision.HIGHEST) * scale_factor
    masked = jnp.where(causal, scores, -jnp.inf)
    row_peak = lax.optimization_barrier(jnp.max(masked, axis=1, keepdims=True))
    exponent = jnp.where(causal, jnp.exp(masked - row_peak), 0.0)
    teacher = exponent / lax.optimization_barrier(jnp.sum(exponent, axis=1, keepdims=True))
    log_gap = jnp.where(causal, cum_rows[:, None] - cum_rows[None, :], -jnp.inf)
    decays = jnp.exp(log_gap)
    student = jnp.dot(c_rows, b_rows.T, precision=lax.Precision.HIGHEST) * decays
    mismatch = student - teacher
    weighted = 2.0 * mismatch * decays
    weighted = lax.optimization_barrier(weighted.astype(jnp.bfloat16)).astype(jnp.float32)
    grad_rows = jnp.dot(weighted, b_rows, precision=lax.Precision.HIGHEST)
    grad_keys = jnp.dot(weighted.T, c_rows, precision=lax.Precision.HIGHEST)
    return (jnp.sum(mismatch * mismatch), grad_rows, grad_keys)

def reference(queries, keys, c_proj, b_proj, log_decay):
    length, heads_all, head_size = queries.shape
    groups = keys.shape[1]
    per_group = heads_all // groups
    cumulative = jnp.cumsum(log_decay, axis=0)

    def one_head(head_index):
        group_index = head_index // per_group
        query_rows = lax.dynamic_index_in_dim(queries, head_index, 1, keepdims=False).astype(jnp.float32)
        c_rows = lax.dynamic_index_in_dim(c_proj, head_index, 1, keepdims=False).astype(jnp.float32)
        key_rows = lax.dynamic_index_in_dim(keys, group_index, 1, keepdims=False).astype(jnp.float32)
        b_rows = lax.dynamic_index_in_dim(b_proj, group_index, 1, keepdims=False).astype(jnp.float32)
        cum_rows = lax.dynamic_index_in_dim(cumulative, head_index, 1, keepdims=False)
        return head_terms(query_rows, key_rows, c_rows, b_rows, cum_rows)
    losses, grad_rows, grad_keys = lax.map(one_head, jnp.arange(heads_all, dtype=jnp.int32))
    distill_loss = jnp.sum(losses) / (heads_all * length)
    grad_c = jnp.transpose(grad_rows, (1, 0, 2))
    grad_b = jnp.transpose(grad_keys.reshape(groups, per_group, length, head_size).sum(axis=1), (1, 0, 2))
    return (distill_loss, grad_c, grad_b)
```

```python
import functools
import math

import jax
import jax.numpy as jnp
from jax import lax
from jax.experimental import pallas as pl
from jax.experimental.pallas import tpu as pltpu
from jax.sharding import PartitionSpec as P

NEG = -1e30
LOG2E = math.log2(math.e)
VMEM = 56 * 1024 * 1024


def dot(a, b):
    return jnp.dot(a, b, preferred_element_type=jnp.float32)


def dot_nt(a, b):
    return lax.dot_general(a, b, (((1,), (1,)), ((), ())), preferred_element_type=jnp.float32)


def pieces(x):
    high = x.astype(jnp.bfloat16)
    rest = x - high.astype(jnp.float32)
    mid = rest.astype(jnp.bfloat16)
    return high, mid, (rest - mid.astype(jnp.float32)).astype(jnp.bfloat16)


def block_kernel(keys, b_rows, log_decay, out, decay_rows):
    fill = jnp.zeros((128, 128 - log_decay.shape[1]), jnp.float32)
    wide = jnp.concatenate([log_decay[...], fill], axis=1)
    for i, part in enumerate(pieces(wide)):
        decay_rows[i] = part
    high, mid, low = pieces(wide.T[0:8])
    down = jnp.concatenate([high, mid, low, jnp.zeros((8, 128), jnp.bfloat16)], axis=0)
    for k in range(out.shape[0]):
        out[k, 0:128] = keys[...]
        out[k, 128:256] = b_rows[...]
        out[k, 256:288] = down


def final_kernel(back, grad_b, lost):
    total = back[0]
    for k in range(1, back.shape[0]):
        total = total + back[k]
    grad_b[...] = 2.0 * total[0:128].T
    for k in range(lost.shape[0]):
        lost[k] = total[128:136]


def pair_of(got, p, first):
    return jnp.concatenate([got[2 * p, first : first + 128], got[2 * p + 1, first : first + 128]], axis=0)


def position(core, row):
    return (row + core * 128) % 256


def causal_mask(place, p, rows):
    chip, core = place[0], place[1]
    row = position(core, lax.broadcasted_iota(jnp.int32, (rows, 256), 0)) + chip * 256
    lane = lax.broadcasted_iota(jnp.int32, (rows, 256), 1)
    key = (2 * p + lane // 128) * 256 + core * 128 + lane % 128
    return row >= key


def stats_kernel(heads, scale2, place, got, own_q, other_q, out, peak, total):
    chip = place[0]
    rows = 2 * own_q.shape[1]
    peak[...] = jnp.full_like(peak, NEG)
    total[...] = jnp.zeros_like(total)

    def step(p, masked):
        keys = pair_of(got, p, 0)
        causal = causal_mask(place, p, rows) if masked else None
        for h in range(heads):
            s = dot_nt(jnp.concatenate([own_q[h], other_q[h]], axis=0), keys)
            if masked:
                s = jnp.where(causal, s, NEG)
            a, b = s[:, :128], s[:, 128:]
            old = peak[h]
            new = jnp.maximum(old, jnp.maximum(a, b))
            total[h] = (
                total[h] * jnp.exp2((old - new) * scale2)
                + jnp.exp2((a - new) * scale2)
                + jnp.exp2((b - new) * scale2)
            )
            peak[h] = new

    full = chip // 2

    @pl.loop(0, full)
    def _(p):
        step(p, False)

    step(full, True)
    lane = lax.broadcasted_iota(jnp.int32, (rows, 128), 1)
    result = jnp.zeros((rows, 128), jnp.float32)
    for h in range(heads):
        top = jnp.max(peak[h], axis=1, keepdims=True)
        summed = jnp.sum(total[h] * jnp.exp2((peak[h] - top) * scale2), axis=1, keepdims=True)
        result = jnp.where(lane == h, top, result)
        result = jnp.where(lane == heads + h, summed, result)
    out[:rows] = result
    blocks = got.shape[0]
    ones = jnp.ones((128, 128), jnp.bfloat16)
    for k in range(blocks):
        sums = dot(got[k, 256:288], ones)
        sums = sums[0:8] + sums[8:16] + sums[16:24]
        out[rows + 8 * k : rows + 8 * k + 8] = sums


def grad_kernel(heads, scale2, place, got, own_q, other_q, own_c, other_c, own_t, other_t, own_s, other_s, own_d, other_d,
                own_grad, other_grad, grad_b, loss, peak, inverse, fade, key_fade):
    chip, core = place[0], place[1]
    rows = 2 * own_q.shape[1]
    half = own_q.shape[1]
    blocks = got.shape[0]
    mine = own_s[:rows]
    theirs = jnp.concatenate([other_s[half:rows], other_s[:half]], axis=0)
    for h in range(heads):
        a, b = mine[:, h : h + 1], theirs[:, h : h + 1]
        top = jnp.maximum(a, b)
        summed = mine[:, heads + h : heads + h + 1] * jnp.exp2((a - top) * scale2) + theirs[
            :, heads + h : heads + h + 1
        ] * jnp.exp2((b - top) * scale2)
        peak[h] = jnp.broadcast_to(top, (rows, 128))
        inverse[h] = jnp.broadcast_to(1.0 / summed, (rows, 128))
    u = lax.broadcasted_iota(jnp.int32, (rows, rows), 0)
    v = lax.broadcasted_iota(jnp.int32, (rows, rows), 1)
    lower = jnp.where(position(core, u) >= position(core, v), 1.0, 0.0).astype(jnp.bfloat16)
    log_rows = jnp.zeros((rows, 128), jnp.float32)
    for i in range(3):
        log_rows = log_rows + dot(lower, jnp.concatenate([own_d[i], other_d[i]], axis=0))
    log_rows = log_rows * LOG2E
    for h in range(heads):
        fade[h] = jnp.broadcast_to(log_rows[:, h : h + 1], (rows, 128))
    u = lax.broadcasted_iota(jnp.int32, (128, 128), 0)
    v = lax.broadcasted_iota(jnp.int32, (128, 128), 1)
    after = jnp.where(u > v, 1.0, 0.0).astype(jnp.bfloat16)
    upto = jnp.where(u <= v, 1.0, 0.0).astype(jnp.bfloat16)
    behind = jnp.zeros((8, 128), jnp.float32)
    for k in range(blocks - 1, -1, -1):
        own_sum, other_sum = (x[rows + 8 * k : rows + 8 * k + 8] for x in (own_s, other_s))
        tail = dot(got[k, 256:288], after)
        tail = tail[0:8] + tail[8:16] + tail[16:24]
        tail = tail + jnp.where(core == 0, other_sum, 0.0) + behind
        head = dot(got[k, 256:288], upto)
        head = head[0:8] + head[8:16] + head[16:24]
        head = head + jnp.where(core == 0, 0.0, other_sum)
        key_fade[k] = jnp.where(chip > k, tail, -head) * LOG2E
        behind = behind + jnp.where(chip > k, own_sum + other_sum, 0.0)

    own_grad[...] = jnp.zeros_like(own_grad)
    other_grad[...] = jnp.zeros_like(other_grad)
    loss[...] = jnp.zeros_like(loss)

    def step(p, masked):
        keys, b_keys = pair_of(got, p, 0), pair_of(got, p, 128)
        causal = causal_mask(place, p, rows) if masked else None
        total_b = jnp.zeros((128, 256), jnp.float32)
        lost = jnp.zeros((8, 128), jnp.float32)
        for h in range(heads):
            s = dot_nt(jnp.concatenate([own_q[h], other_q[h]], axis=0), keys)
            inner = dot_nt(jnp.concatenate([own_c[h], other_c[h]], axis=0), b_keys)
            top = jnp.concatenate([peak[h], peak[h]], axis=1)
            inv = jnp.concatenate([inverse[h], inverse[h]], axis=1)
            teacher = jnp.exp2((s - top) * scale2) * inv
            row_log = jnp.concatenate([fade[h], fade[h]], axis=1)
            key_log = jnp.concatenate([key_fade[2 * p, h : h + 1], key_fade[2 * p + 1, h : h + 1]], axis=1)
            if masked:
                decay = jnp.exp2(jnp.where(causal, row_log + key_log, NEG))
                teacher = jnp.where(causal, teacher, 0.0)
            else:
                decay = jnp.exp2(row_log + key_log)
            mismatch = inner * decay - teacher
            square = mismatch * mismatch
            lost = lost + jnp.sum(square.reshape(rows // 8, 8, 256), axis=0)[:, :128]
            lost = lost + jnp.sum(square.reshape(rows // 8, 8, 256), axis=0)[:, 128:]
            weighted = (mismatch * decay).astype(jnp.bfloat16)
            part = dot(weighted, b_keys)
            own_grad[h] += part[:half]
            other_grad[h] += part[half:]
            total_b = total_b + dot(jnp.concatenate([own_t[h], other_t[h]], axis=1), weighted)
        loss[...] += lost
        grad_b[2 * p] = total_b[:, :128]
        grad_b[2 * p + 1] = total_b[:, 128:]

    full = chip // 2

    @pl.loop(0, full)
    def _(p):
        step(p, False)

    step(full, True)

    @pl.loop(full + 1, blocks // 2)
    def _(p):
        grad_b[2 * p] = jnp.zeros((128, 128), jnp.float32)
        grad_b[2 * p + 1] = jnp.zeros((128, 128), jnp.float32)


def shards(queries, keys, c_proj, b_proj, log_decay):
    rows_dev, heads, size = queries.shape
    peers = lax.axis_size("context")
    chips = peers // 2
    rows = 2 * rows_dev
    here = lax.axis_index("context")
    core = here % 2
    place = jnp.stack([here // 2, core]).astype(jnp.int32)
    scale2 = LOG2E / math.sqrt(size)
    plane = [[2 * k + c for k in range(chips)] for c in range(2)]
    swap = [(i, i ^ 1) for i in range(peers)]

    f32 = functools.partial(jax.ShapeDtypeStruct, dtype=jnp.float32)
    bf16 = functools.partial(jax.ShapeDtypeStruct, dtype=jnp.bfloat16)
    smem = pl.BlockSpec(memory_space=pltpu.SMEM)
    vmem = pl.BlockSpec(memory_space=pltpu.VMEM)
    params = pltpu.CompilerParams(vmem_limit_bytes=VMEM)
    work = heads * rows * chips * 128

    block, own_d = pl.pallas_call(
        block_kernel,
        out_shape=(bf16((chips, 288, 128)), bf16((3, rows_dev, 128))),
        in_specs=[vmem] * 3,
        out_specs=(vmem,) * 2,
        compiler_params=params,
        name="block",
    )(keys[:, 0], b_proj[:, 0], log_decay)
    got = lax.all_to_all(block, "context", 0, 0, axis_index_groups=plane)

    own_q, own_c, own_t = queries.transpose(1, 0, 2), c_proj.transpose(1, 0, 2), c_proj.transpose(1, 2, 0)
    other_q, other_c, other_t, other_d = (lax.ppermute(x, "context", swap) for x in (own_q, own_c, own_t, own_d))

    own_s = pl.pallas_call(
        functools.partial(stats_kernel, heads, scale2),
        out_shape=f32((rows + 8 * chips, 128)),
        in_specs=[smem] + [vmem] * 3,
        out_specs=vmem,
        scratch_shapes=[pltpu.VMEM((heads, rows, 128), jnp.float32)] * 2,
        compiler_params=params,
        cost_estimate=pl.CostEstimate(flops=2 * work * size, bytes_accessed=2 << 20, transcendentals=work),
        name="stats",
    )(place, got, own_q, other_q)
    other_s = lax.ppermute(own_s, "context", swap)

    own_grad, other_grad, grad_b, loss = pl.pallas_call(
        functools.partial(grad_kernel, heads, scale2),
        out_shape=(f32((heads, rows_dev, size)),) * 2 + (f32((chips, size, 128)), f32((8, 128))),
        in_specs=[smem] + [vmem] * 11,
        out_specs=(vmem,) * 4,
        scratch_shapes=[pltpu.VMEM((heads, rows, 128), jnp.float32)] * 3 + [pltpu.VMEM((chips, 8, 128), jnp.float32)],
        compiler_params=params,
        cost_estimate=pl.CostEstimate(flops=8 * work * size, bytes_accessed=6 << 20, transcendentals=2 * work),
        name="grads",
    )(place, got, own_q, other_q, own_c, other_c, own_t, other_t, own_s, other_s, own_d, other_d)

    lost = jnp.broadcast_to(jnp.sum(loss), (chips, 8, 128))
    sent = jnp.concatenate([grad_b, lost], axis=1)
    back = lax.all_to_all(sent, "context", 0, 0, axis_index_groups=plane)
    grad_c = (2.0 * (own_grad + lax.ppermute(other_grad, "context", swap))).transpose(1, 0, 2)
    z_size = lax.axis_size("head")
    mine, lost = pl.pallas_call(
        final_kernel,
        out_shape=(f32((rows_dev, size)), f32((2 * z_size, 8, 128))),
        in_specs=[vmem],
        out_specs=(vmem,) * 2,
        compiler_params=params,
        name="final",
    )(back)

    columns = [[(2 * k + c) * z_size + z for c in range(2) for z in range(z_size)] for k in range(chips)]
    lost = lax.all_to_all(lost, ("context", "head"), 0, 0, axis_index_groups=columns)
    distill_loss = jnp.sum(lost[:, 0, 0]) / (heads * z_size * peers * rows_dev)
    return distill_loss, grad_c, mine[:, None, :]


def solution(mesh):
    in_specs = (
        P("context", "head", None),
        P("context", "head", None),
        P("context", "head", None),
        P("context", "head", None),
        P("context", "head"),
    )
    out_specs = (P(), P("context", "head", None), P("context", "head", None))
    return jax.shard_map(shards, mesh=mesh, in_specs=in_specs, out_specs=out_specs, check_vma=False)
```

```python
import functools
import math

import jax
import jax.numpy as jnp
from jax import lax
from jax.experimental import pallas as pl
from jax.experimental.pallas import tpu as pltpu
from jax.sharding import PartitionSpec as P

NEG = -1e30
LOG2E = math.log2(math.e)
TINY = 1e-30
SMALL, STATS, GRADS = 8 << 20, 24 << 20, 32 << 20


def dot(a, b):
    return jnp.dot(a, b, preferred_element_type=jnp.float32)


def dot_nt(a, b):
    return lax.dot_general(a, b, (((1,), (1,)), ((), ())), preferred_element_type=jnp.float32)


def pieces(x):
    high = x.astype(jnp.bfloat16)
    rest = x - high.astype(jnp.float32)
    mid = rest.astype(jnp.bfloat16)
    return high, mid, (rest - mid.astype(jnp.float32)).astype(jnp.bfloat16)


def exponent(x):
    return jnp.floor(jnp.log2(jnp.maximum(x, TINY)))


def position(core, row):
    return (row + core * 128) % 256


def block_kernel(keys, b_rows, log_decay, out):
    high, mid, low = pieces(log_decay[...])
    down = jnp.concatenate([high, mid, low, jnp.zeros((8, 128), jnp.bfloat16)], axis=0)
    key_cols, b_cols = keys[...].T, b_rows[...].T
    for k in range(out.shape[0]):
        out[k, 0:128] = key_cols
        out[k, 128:256] = b_cols
        out[k, 256:288] = down


def stats_kernel(heads, scale2, place, got, own_q, other_q, log_decay, out):
    chip, core = place[0], place[1]
    blocks = got.shape[0]
    half = own_q.shape[1]
    rows = 2 * half
    row = lax.broadcasted_iota(jnp.int32, (rows, 128), 0)
    lane = lax.broadcasted_iota(jnp.int32, (rows, 128), 1)
    gap = position(core, row) - lane - core * 128 + chip * 256
    keys = jnp.concatenate([got[k, 0:128] for k in range(blocks)], axis=1)
    result = jnp.zeros((rows, 128), jnp.float32)
    for h in range(heads):
        s = dot(jnp.concatenate([own_q[h], other_q[h]], axis=0), keys)
        parts = [jnp.where(gap >= 256 * k, s[:, 128 * k : 128 * k + 128], NEG) for k in range(blocks)]
        top = jnp.max(functools.reduce(jnp.maximum, parts), axis=1, keepdims=True)
        summed = jnp.sum(sum(jnp.exp2((x - top) * scale2) for x in parts), axis=1, keepdims=True)
        result = jnp.where(lane == h, top, result)
        result = jnp.where(lane == heads + h, summed, result)
    out[:rows] = result
    ones = jnp.ones((128, 128), jnp.bfloat16)
    for k in range(blocks):
        sums = dot(got[k, 256:288], ones)
        out[rows + 8 * k : rows + 8 * k + 8] = sums[0:8] + sums[8:16] + sums[16:24]
    wide = jnp.concatenate([log_decay[...], jnp.zeros((128 - heads, 128), jnp.float32)], axis=0)
    out[rows + 8 * blocks :] = wide.T


def grad_kernel(heads, scale2, group, place, got, own_q, other_q, own_c, other_c, own_t, other_t, own_s, other_s,
                own_grad, other_grad, sent, peak, fade, log_fade, key_fade, key_log, weighted, loss):
    chip, core = place[0], place[1]
    half = own_s.shape[0] // 4
    rows = 2 * half
    blocks = got.shape[0]
    tiles = 2 * heads
    width = group * 128
    mine = own_s[:rows]
    theirs = jnp.concatenate([other_s[half:rows], other_s[:half]], axis=0)
    u = lax.broadcasted_iota(jnp.int32, (rows, rows), 0)
    v = lax.broadcasted_iota(jnp.int32, (rows, rows), 1)
    lower = jnp.where(position(core, u) >= position(core, v), 1.0, 0.0).astype(jnp.bfloat16)
    log_rows = jnp.zeros((rows, 128), jnp.float32)
    for part in pieces(jnp.concatenate([own_s[rows + 8 * blocks :], other_s[rows + 8 * blocks :]], axis=0)):
        log_rows = log_rows + dot(lower, part)
    log_rows = log_rows * LOG2E
    for h in range(heads):
        a, b = mine[:, h : h + 1], theirs[:, h : h + 1]
        top = jnp.maximum(a, b)
        summed = mine[:, heads + h : heads + h + 1] * jnp.exp2((a - top) * scale2) + theirs[
            :, heads + h : heads + h + 1
        ] * jnp.exp2((b - top) * scale2)
        level = jnp.broadcast_to(top * scale2 + jnp.log2(summed), (rows, 128))
        row_log = jnp.broadcast_to(log_rows[:, h : h + 1], (rows, 128))
        row_fade = jnp.exp2(row_log)
        for t, first in ((h, 0), (heads + h, half)):
            peak[t] = level[first : first + half]
            log_fade[t] = row_log[first : first + half]
            fade[t] = row_fade[first : first + half]
    u = lax.broadcasted_iota(jnp.int32, (128, 128), 0)
    v = lax.broadcasted_iota(jnp.int32, (128, 128), 1)
    after = jnp.where(u > v, 1.0, 0.0).astype(jnp.bfloat16)
    upto = jnp.where(u <= v, 1.0, 0.0).astype(jnp.bfloat16)
    behind = jnp.zeros((8, 128), jnp.float32)
    for k in range(blocks - 1, -1, -1):
        own_sum, other_sum = (x[rows + 8 * k : rows + 8 * k + 8] for x in (own_s, other_s))
        tail = dot(got[k, 256:288], after)
        tail = tail[0:8] + tail[8:16] + tail[16:24]
        tail = tail + jnp.where(core == 0, other_sum, 0.0) + behind
        head = dot(got[k, 256:288], upto)
        head = head[0:8] + head[8:16] + head[16:24]
        head = head + jnp.where(core == 0, 0.0, other_sum)
        logs = jnp.where(chip > k, tail, -head) * LOG2E
        key_log[k] = logs
        key_fade[k] = jnp.exp2(jnp.minimum(logs, 0.0))
        behind = behind + jnp.where(chip > k, own_sum + other_sum, 0.0)

    own_grad[...] = jnp.zeros_like(own_grad)
    other_grad[...] = jnp.zeros_like(other_grad)
    loss[...] = jnp.zeros_like(loss)
    row = lax.broadcasted_iota(jnp.int32, (half, 128), 0)
    lane = lax.broadcasted_iota(jnp.int32, (half, 128), 1)
    gaps = [position(core, row + first) - lane - core * 128 for first in (0, half)]

    def step(p, masked):
        keys = jnp.concatenate([got[group * p + i, 0:128] for i in range(group)], axis=1)
        b_cols = jnp.concatenate([got[group * p + i, 128:256] for i in range(group)], axis=1)
        lost = jnp.zeros((8, 128), jnp.float32)
        for side, (q, c) in enumerate(((own_q, own_c), (other_q, other_c))):
            scores = dot(q[...].reshape(heads * half, 128), keys)
            inner = dot(c[...].reshape(heads * half, 128), b_cols)
            for h in range(heads):
                t = side * heads + h
                at = slice(h * half, h * half + half)
                for i in range(group):
                    to = slice(128 * i, 128 * i + 128)
                    k = group * p + i
                    s = scores[at, to] * scale2
                    if masked:
                        causal = gaps[side] >= (k - chip) * 256
                        teacher = jnp.exp2(jnp.where(causal, s - peak[t], NEG))
                        decay = jnp.exp2(jnp.where(causal, log_fade[t] + key_log[k, h : h + 1], NEG))
                    else:
                        teacher = jnp.exp2(s - peak[t])
                        decay = fade[t] * key_fade[k, h : h + 1]
                    mismatch = inner[at, to] * decay - teacher
                    square = mismatch * mismatch
                    lost = lost + jnp.sum(square.reshape(half // 8, 8, 128), axis=0)
                    weighted[t * half : t * half + half, to] = (mismatch * decay).astype(jnp.bfloat16)
        loss[...] += lost
        parts = dot_nt(b_cols, weighted[...])
        own_grad[...] += parts[:, : heads * half]
        other_grad[...] += parts[:, heads * half :]
        parts = dot(own_t[...], weighted[: heads * half]) + dot(other_t[...], weighted[heads * half :])
        for i in range(group):
            sent[group * p + i, 0:128] = parts[:, 128 * i : 128 * i + 128]

    full = chip // group

    @pl.loop(0, full)
    def _(p):
        step(p, False)

    step(full, True)

    @pl.loop(group * (full + 1), blocks)
    def _(k):
        sent[k, 0:128] = jnp.zeros((128, 128), jnp.float32)

    top = functools.reduce(jnp.maximum, [jnp.abs(sent[k, 0:128]) for k in range(blocks)])
    power = exponent(jnp.broadcast_to(jnp.max(top, keepdims=True), (16, 128)))
    total = jnp.broadcast_to(jnp.sum(loss[...], keepdims=True), (16, 128))
    lost_power = exponent(total)
    share = total * jnp.exp2(-lost_power)
    coarse = jnp.floor(share * 1024.0) * (1.0 / 1024.0)
    lane = lax.broadcasted_iota(jnp.int32, (16, 128), 1)
    extra = jnp.where(lane == 0, power, 0.0)
    extra = jnp.where(lane == 1, lost_power, extra)
    extra = jnp.where(lane == 2, coarse, extra)
    extra = jnp.where(lane == 3, (share - coarse) * 1024.0, extra)
    up = jnp.broadcast_to(jnp.exp2(13.0 - power)[0:1], (128, 128))
    for k in range(blocks):
        sent[k, 0:128] = sent[k, 0:128] * up
        sent[k, 128:144] = extra


def final_kernel(back, grad_b, lost):
    blocks = back.shape[0]
    total = jnp.zeros((128, 128), jnp.float32)
    loss = jnp.zeros((1, 128), jnp.float32)
    for k in range(blocks):
        extra = back[k, 128:129]
        power = jnp.broadcast_to(extra[:, 0:1], (1, 128))
        total = total + back[k, 0:128] * jnp.exp2(power - 13.0)
        share = extra[:, 2:3] + extra[:, 3:4] * (1.0 / 1024.0)
        loss = loss + jnp.broadcast_to(share * jnp.exp2(extra[:, 1:2]), (1, 128))
    grad_b[...] = 2.0 * total.T
    for k in range(lost.shape[0]):
        lost[k] = jnp.broadcast_to(loss, (8, 128))


def shards(queries, keys, c_proj, b_proj, log_decay):
    rows_dev, heads, size = queries.shape
    peers = lax.axis_size("context")
    z_size = lax.axis_size("head")
    chips = peers // 2
    rows = 2 * rows_dev
    group = 4
    here = lax.axis_index("context")
    place = jnp.stack([here // 2, here % 2]).astype(jnp.int32)
    scale2 = LOG2E / math.sqrt(size)
    plane = [[2 * k + c for k in range(chips)] for c in range(2)]
    swap = [(i, i ^ 1) for i in range(peers)]

    f32 = functools.partial(jax.ShapeDtypeStruct, dtype=jnp.float32)
    bf16 = functools.partial(jax.ShapeDtypeStruct, dtype=jnp.bfloat16)
    smem = pl.BlockSpec(memory_space=pltpu.SMEM)
    vmem = pl.BlockSpec(memory_space=pltpu.VMEM)
    work = heads * rows * chips * 128

    down = log_decay.T
    block = pl.pallas_call(
        block_kernel,
        out_shape=bf16((chips, 288, 128)),
        in_specs=[vmem] * 3,
        out_specs=vmem,
        compiler_params=pltpu.CompilerParams(vmem_limit_bytes=SMALL),
        name="block",
    )(keys[:, 0], b_proj[:, 0], down)
    got = lax.all_to_all(block, "context", 0, 0, axis_index_groups=plane)

    own_q, own_c = queries.transpose(1, 0, 2), c_proj.transpose(1, 0, 2)
    own_t = c_proj.transpose(2, 1, 0).reshape(size, heads * rows_dev)
    other_q, other_c, other_t = (lax.ppermute(x, "context", swap) for x in (own_q, own_c, own_t))

    own_s = pl.pallas_call(
        functools.partial(stats_kernel, heads, scale2),
        out_shape=f32((rows + 8 * chips + 128, 128)),
        in_specs=[smem] + [vmem] * 4,
        out_specs=vmem,
        compiler_params=pltpu.CompilerParams(vmem_limit_bytes=STATS),
        cost_estimate=pl.CostEstimate(flops=2 * work * size, bytes_accessed=2 << 20, transcendentals=work),
        name="stats",
    )(place, got, own_q, other_q, down)
    other_s = lax.ppermute(own_s, "context", swap)

    own_grad, other_grad, sent = pl.pallas_call(
        functools.partial(grad_kernel, heads, scale2, group),
        out_shape=(f32((size, heads * rows_dev)),) * 2 + (f32((chips, 144, 128)),),
        in_specs=[smem] + [vmem] * 9,
        out_specs=(vmem,) * 3,
        scratch_shapes=[pltpu.VMEM((2 * heads, rows_dev, 128), jnp.float32)] * 3
        + [pltpu.VMEM((chips, 8, 128), jnp.float32)] * 2
        + [pltpu.VMEM((heads * rows, group * 128), jnp.bfloat16), pltpu.VMEM((8, 128), jnp.float32)],
        compiler_params=pltpu.CompilerParams(vmem_limit_bytes=GRADS),
        cost_estimate=pl.CostEstimate(flops=8 * work * size, bytes_accessed=6 << 20, transcendentals=2 * work),
        name="grads",
    )(place, got, own_q, other_q, own_c, other_c, own_t, other_t, own_s, other_s)

    back = lax.all_to_all(sent.astype(jnp.float16), "context", 0, 0, axis_index_groups=plane)
    grad_c = 2.0 * (own_grad + lax.ppermute(other_grad, "context", swap))
    grad_c = grad_c.reshape(size, heads, rows_dev).transpose(2, 1, 0)
    mine, lost = pl.pallas_call(
        final_kernel,
        out_shape=(f32((rows_dev, size)), f32((2 * z_size, 8, 128))),
        in_specs=[vmem],
        out_specs=(vmem,) * 2,
        compiler_params=pltpu.CompilerParams(vmem_limit_bytes=SMALL),
        name="final",
    )(back.astype(jnp.float32))

    columns = [[(2 * k + c) * z_size + z for c in range(2) for z in range(z_size)] for k in range(chips)]
    lost = lax.all_to_all(lost, ("context", "head"), 0, 0, axis_index_groups=columns)
    distill_loss = jnp.sum(lost[:, 0, 0]) / (heads * z_size * peers * rows_dev)
    return distill_loss, grad_c, mine[:, None, :]


def solution(mesh):
    in_specs = (
        P("context", "head", None),
        P("context", "head", None),
        P("context", "head", None),
        P("context", "head", None),
        P("context", "head"),
    )
    out_specs = (P(), P("context", "head", None), P("context", "head", None))
    return jax.shard_map(shards, mesh=mesh, in_specs=in_specs, out_specs=out_specs, check_vma=False)
```

```python
import functools
import math

import jax
import jax.numpy as jnp
from jax import lax
from jax.experimental import pallas as pl
from jax.experimental.pallas import tpu as pltpu
from jax.sharding import PartitionSpec as P

NEG = -1e30
LOG2E = math.log2(math.e)
TINY = 1e-30
FULL, SMALL, STATS, GRADS = 60 << 20, 8 << 20, 16 << 20, 20 << 20


def dot(a, b):
    return jnp.dot(a, b, preferred_element_type=jnp.float32)


def dot_nt(a, b):
    return lax.dot_general(a, b, (((1,), (1,)), ((), ())), preferred_element_type=jnp.float32)


def pieces(x):
    high = x.astype(jnp.bfloat16)
    rest = x - high.astype(jnp.float32)
    mid = rest.astype(jnp.bfloat16)
    return high, mid, (rest - mid.astype(jnp.float32)).astype(jnp.bfloat16)


def exponent(x):
    return jnp.floor(jnp.log2(jnp.maximum(x, TINY)))


def position(core, row):
    return (row + core * 128) % 256


def block_kernel(keys, b_rows, log_decay, out):
    high, mid, low = pieces(log_decay[...])
    down = jnp.concatenate([high, mid, low, jnp.zeros((8, 128), jnp.bfloat16)], axis=0)
    key_cols, b_cols = keys[...].T, b_rows[...].T
    for k in range(out.shape[0]):
        out[k, 0:128] = key_cols
        out[k, 128:256] = b_cols
        out[k, 256:288] = down


def stats_kernel(heads, scale2, group, place, got, own_q, other_q, log_decay, out, scores):
    chip, core = place[0], place[1]
    blocks = got.shape[0]
    half = own_q.shape[1]
    rows = 2 * half
    row = lax.broadcasted_iota(jnp.int32, (rows, 128), 0)
    lane = lax.broadcasted_iota(jnp.int32, (rows, 128), 1)
    gap = position(core, row) - lane - core * 128 + chip * 256
    keys = jnp.concatenate([got[k, 0:128] for k in range(blocks)], axis=1)
    result = jnp.zeros((rows, 128), jnp.float32)
    width = 128 * group
    for h in range(heads):
        s = dot(jnp.concatenate([own_q[h], other_q[h]], axis=0), keys) * scale2
        for p in range(blocks // group):
            scores[p, h * half : h * half + half] = s[:half, width * p : width * p + width]
            scores[p, (heads + h) * half : (heads + h) * half + half] = s[half:, width * p : width * p + width]
        parts = [jnp.where(gap >= 256 * k, s[:, 128 * k : 128 * k + 128], NEG) for k in range(blocks)]
        top = jnp.max(functools.reduce(jnp.maximum, parts), axis=1, keepdims=True)
        summed = jnp.sum(sum(jnp.exp2(x - top) for x in parts), axis=1, keepdims=True)
        result = jnp.where(lane == h, top, result)
        result = jnp.where(lane == heads + h, summed, result)
    out[:rows] = result
    ones = jnp.ones((128, 128), jnp.bfloat16)
    for k in range(blocks):
        sums = dot(got[k, 256:288], ones)
        out[rows + 8 * k : rows + 8 * k + 8] = sums[0:8] + sums[8:16] + sums[16:24]
    wide = jnp.concatenate([log_decay[...], jnp.zeros((128 - heads, 128), jnp.float32)], axis=0)
    out[rows + 8 * blocks :] = wide.T


def mismatch_kernel(heads, group, place, got, scores, own_c, other_c, own_s, other_s, weighted, loss,
                    peak, fade, log_fade, key_fade, key_log, total):
    chip, core = place[0], place[1]
    half = own_s.shape[0] // 4
    rows = 2 * half
    blocks = got.shape[0]
    mine = own_s[:rows]
    theirs = jnp.concatenate([other_s[half:rows], other_s[:half]], axis=0)
    u = lax.broadcasted_iota(jnp.int32, (rows, rows), 0)
    v = lax.broadcasted_iota(jnp.int32, (rows, rows), 1)
    lower = jnp.where(position(core, u) >= position(core, v), 1.0, 0.0).astype(jnp.bfloat16)
    log_rows = jnp.zeros((rows, 128), jnp.float32)
    for part in pieces(jnp.concatenate([own_s[rows + 8 * blocks :], other_s[rows + 8 * blocks :]], axis=0)):
        log_rows = log_rows + dot(lower, part)
    log_rows = log_rows * LOG2E
    for h in range(heads):
        a, b = mine[:, h : h + 1], theirs[:, h : h + 1]
        top = jnp.maximum(a, b)
        summed = mine[:, heads + h : heads + h + 1] * jnp.exp2(a - top) + theirs[
            :, heads + h : heads + h + 1
        ] * jnp.exp2(b - top)
        level = jnp.broadcast_to(top + jnp.log2(summed), (rows, 128))
        row_log = jnp.broadcast_to(log_rows[:, h : h + 1], (rows, 128))
        row_fade = jnp.exp2(row_log)
        for t, first in ((h, 0), (heads + h, half)):
            peak[t] = level[first : first + half]
            log_fade[t] = row_log[first : first + half]
            fade[t] = row_fade[first : first + half]
    u = lax.broadcasted_iota(jnp.int32, (128, 128), 0)
    v = lax.broadcasted_iota(jnp.int32, (128, 128), 1)
    after = jnp.where(u > v, 1.0, 0.0).astype(jnp.bfloat16)
    upto = jnp.where(u <= v, 1.0, 0.0).astype(jnp.bfloat16)
    behind = jnp.zeros((8, 128), jnp.float32)
    for k in range(blocks - 1, -1, -1):
        own_sum, other_sum = (x[rows + 8 * k : rows + 8 * k + 8] for x in (own_s, other_s))
        tail = dot(got[k, 256:288], after)
        tail = tail[0:8] + tail[8:16] + tail[16:24]
        tail = tail + jnp.where(core == 0, other_sum, 0.0) + behind
        head = dot(got[k, 256:288], upto)
        head = head[0:8] + head[8:16] + head[16:24]
        head = head + jnp.where(core == 0, 0.0, other_sum)
        logs = jnp.where(chip > k, tail, -head) * LOG2E
        key_log[k] = logs
        key_fade[k] = jnp.exp2(jnp.minimum(logs, 0.0))
        behind = behind + jnp.where(chip > k, own_sum + other_sum, 0.0)

    total[...] = jnp.zeros_like(total)
    row = lax.broadcasted_iota(jnp.int32, (half, 128), 0)
    lane = lax.broadcasted_iota(jnp.int32, (half, 128), 1)
    gaps = [position(core, row + first) - lane - core * 128 for first in (0, half)]

    def wide(x):
        return jnp.concatenate([x] * group, axis=1)

    def step(p, masked):
        places = [group * p + i for i in range(group)]
        b_cols = jnp.concatenate([got[k, 128:256] for k in places], axis=1)
        lost = jnp.zeros((8, 128), jnp.float32)
        for side, c in enumerate((own_c, other_c)):
            inner = dot(c[...].reshape(heads * half, 128), b_cols)
            if masked:
                causal = jnp.concatenate([gaps[side] >= (k - chip) * 256 for k in places], axis=1)
            for h in range(heads):
                t = side * heads + h
                at = slice(t * half, t * half + half)
                from_peak = scores[p, at] - wide(peak[t])
                if masked:
                    logs = wide(log_fade[t]) + jnp.concatenate([key_log[k, h : h + 1] for k in places], axis=1)
                    teacher = jnp.exp2(jnp.where(causal, from_peak, NEG))
                    decay = jnp.exp2(jnp.where(causal, logs, NEG))
                else:
                    teacher = jnp.exp2(from_peak)
                    decay = wide(fade[t]) * jnp.concatenate([key_fade[k, h : h + 1] for k in places], axis=1)
                mismatch = inner[h * half : h * half + half] * decay - teacher
                square = jnp.sum((mismatch * mismatch).reshape(half // 8, 8, 128 * group), axis=0)
                for i in range(group):
                    lost = lost + square[:, 128 * i : 128 * i + 128]
                weighted[p, at] = (mismatch * decay).astype(jnp.bfloat16)
        total[...] += lost

    full = chip // group

    @pl.loop(0, full)
    def _(p):
        step(p, False)

    step(full, True)
    lost = jnp.broadcast_to(jnp.sum(total[...], keepdims=True), (8, 128))
    for k in range(loss.shape[0]):
        loss[k] = lost


def grad_kernel(group, place, got, weighted, own_t, other_t, own_grad, other_grad, sent, power):
    blocks = got.shape[0]
    side = own_t.shape[1]
    full = place[0] // group
    own_grad[...] = jnp.zeros_like(own_grad)
    other_grad[...] = jnp.zeros_like(other_grad)

    @pl.loop(0, full + 1)
    def _(p):
        b_cols = jnp.concatenate([got[group * p + i, 128:256] for i in range(group)], axis=1)
        parts = dot_nt(b_cols, weighted[p])
        own_grad[...] += parts[:, :side]
        other_grad[...] += parts[:, side:]
        parts = dot(own_t[...], weighted[p, :side]) + dot(other_t[...], weighted[p, side:])
        for i in range(group):
            sent[group * p + i] = parts[:, 128 * i : 128 * i + 128]

    @pl.loop(group * (full + 1), blocks)
    def _(k):
        sent[k] = jnp.zeros((128, 128), jnp.float32)

    top = functools.reduce(jnp.maximum, [jnp.abs(sent[k]) for k in range(blocks)])
    level = exponent(jnp.broadcast_to(jnp.max(top, keepdims=True), (128, 128)))
    up = jnp.exp2(13.0 - level)
    for k in range(blocks):
        sent[k] = sent[k] * up
    power[...] = level[0:8]


def extra_kernel(lost, power, extra):
    total = lost[0]
    for k in range(1, lost.shape[0]):
        total = total + lost[k]
    lost_power = exponent(total)
    share = total * jnp.exp2(-lost_power)
    coarse = jnp.floor(share * 1024.0) * (1.0 / 1024.0)
    lane = lax.broadcasted_iota(jnp.int32, (8, 128), 1)
    row = jnp.where(lane == 0, power[...], 0.0)
    row = jnp.where(lane == 1, lost_power, row)
    row = jnp.where(lane == 2, coarse, row)
    row = jnp.where(lane == 3, (share - coarse) * 1024.0, row)
    extra[...] = jnp.concatenate([row, row], axis=0)


def final_kernel(count, back, grad_b, mean):
    blocks = back.shape[0]
    total = jnp.zeros((128, 128), jnp.float32)
    loss = jnp.zeros((1, 128), jnp.float32)
    for k in range(blocks):
        extra = back[k, 128:129]
        power = jnp.broadcast_to(extra[:, 0:1], (1, 128))
        total = total + back[k, 0:128] * jnp.exp2(power - 13.0)
        share = extra[:, 2:3] + extra[:, 3:4] * (1.0 / 1024.0)
        loss = loss + jnp.broadcast_to(share * jnp.exp2(extra[:, 1:2]), (1, 128))
    grad_b[...] = 2.0 * total.T
    mean[...] = jnp.broadcast_to(loss * (1.0 / count), (8, 128))


def shards(queries, keys, c_proj, b_proj, log_decay):
    rows_dev, heads, size = queries.shape
    peers = lax.axis_size("context")
    z_size = lax.axis_size("head")
    chips = peers // 2
    rows = 2 * rows_dev
    group = 4
    here = lax.axis_index("context")
    place = jnp.stack([here // 2, here % 2]).astype(jnp.int32)
    scale2 = LOG2E / math.sqrt(size)
    plane = [[2 * k + c for k in range(chips)] for c in range(2)]
    swap = [(i, i ^ 1) for i in range(peers)]

    f32 = functools.partial(jax.ShapeDtypeStruct, dtype=jnp.float32)
    bf16 = functools.partial(jax.ShapeDtypeStruct, dtype=jnp.bfloat16)
    smem = pl.BlockSpec(memory_space=pltpu.SMEM)
    vmem = pl.BlockSpec(memory_space=pltpu.VMEM)
    work = heads * rows * chips * 128

    down = log_decay.T
    block = pl.pallas_call(
        block_kernel,
        out_shape=bf16((chips, 288, 128)),
        in_specs=[vmem] * 3,
        out_specs=vmem,
        compiler_params=pltpu.CompilerParams(vmem_limit_bytes=FULL),
        name="block",
    )(keys[:, 0], b_proj[:, 0], down)
    got = lax.all_to_all(block, "context", 0, 0, axis_index_groups=plane)

    own_q, own_c = queries.transpose(1, 0, 2), c_proj.transpose(1, 0, 2)
    own_t = c_proj.transpose(2, 1, 0).reshape(size, heads * rows_dev)
    other_q, other_c, other_t = (lax.ppermute(x, "context", swap) for x in (own_q, own_c, own_t))

    own_s, scores = pl.pallas_call(
        functools.partial(stats_kernel, heads, scale2, group),
        out_shape=(f32((rows + 8 * chips + 128, 128)), f32((chips // group, heads * rows, 128 * group))),
        in_specs=[smem] + [vmem] * 4,
        out_specs=(vmem,) * 2,
        compiler_params=pltpu.CompilerParams(vmem_limit_bytes=STATS),
        cost_estimate=pl.CostEstimate(flops=2 * work * size, bytes_accessed=2 << 20, transcendentals=work),
        name="stats",
    )(place, got, own_q, other_q, down)
    other_s = lax.ppermute(own_s, "context", swap)

    weighted, lost = pl.pallas_call(
        functools.partial(mismatch_kernel, heads, group),
        out_shape=(bf16((chips // group, heads * rows, 128 * group)), f32((2 * z_size, 8, 128))),
        in_specs=[smem] + [vmem] * 6,
        out_specs=(vmem,) * 2,
        scratch_shapes=[pltpu.VMEM((2 * heads, rows_dev, 128), jnp.float32)] * 3
        + [pltpu.VMEM((chips, 8, 128), jnp.float32)] * 2
        + [pltpu.VMEM((8, 128), jnp.float32)],
        compiler_params=pltpu.CompilerParams(vmem_limit_bytes=GRADS),
        cost_estimate=pl.CostEstimate(flops=2 * work * size, bytes_accessed=4 << 20, transcendentals=2 * work),
        name="mismatch",
    )(place, got, scores, own_c, other_c, own_s, other_s)

    columns = [[(2 * k + c) * z_size + z for c in range(2) for z in range(z_size)] for k in range(chips)]
    lost = lax.all_to_all(lost, ("context", "head"), 0, 0, axis_index_groups=columns)

    own_grad, other_grad, sent, power = pl.pallas_call(
        functools.partial(grad_kernel, group),
        out_shape=(f32((size, heads * rows_dev)),) * 2 + (f32((chips, size, 128)), f32((8, 128))),
        in_specs=[smem] + [vmem] * 4,
        out_specs=(vmem,) * 4,
        compiler_params=pltpu.CompilerParams(vmem_limit_bytes=GRADS),
        cost_estimate=pl.CostEstimate(flops=4 * work * size, bytes_accessed=4 << 20, transcendentals=0),
        name="grads",
    )(place, got, weighted, own_t, other_t)

    extra = pl.pallas_call(
        extra_kernel,
        out_shape=f32((16, 128)),
        in_specs=[vmem] * 2,
        out_specs=vmem,
        compiler_params=pltpu.CompilerParams(vmem_limit_bytes=SMALL),
        name="extra",
    )(lost, power)

    sent = jnp.concatenate([sent, jnp.broadcast_to(extra, (chips, 16, 128))], axis=1)
    back = lax.all_to_all(sent.astype(jnp.float16), "context", 0, 0, axis_index_groups=plane)
    grad_c = 2.0 * (own_grad + lax.ppermute(other_grad, "context", swap))
    grad_c = grad_c.reshape(size, heads, rows_dev).transpose(2, 1, 0)
    mine, mean = pl.pallas_call(
        functools.partial(final_kernel, heads * z_size * peers * rows_dev),
        out_shape=(f32((rows_dev, size)), f32((8, 128))),
        in_specs=[vmem],
        out_specs=(vmem,) * 2,
        compiler_params=pltpu.CompilerParams(vmem_limit_bytes=SMALL),
        name="final",
    )(back.astype(jnp.float32))
    return mean[0, 0], grad_c, mine[:, None, :]


def solution(mesh):
    in_specs = (
        P("context", "head", None),
        P("context", "head", None),
        P("context", "head", None),
        P("context", "head", None),
        P("context", "head"),
    )
    out_specs = (P(), P("context", "head", None), P("context", "head", None))
    return jax.shard_map(shards, mesh=mesh, in_specs=in_specs, out_specs=out_specs, check_vma=False)
```

```python
import functools
import math

import jax
import jax.numpy as jnp
from jax import lax
from jax.experimental import pallas as pl
from jax.experimental.pallas import tpu as pltpu
from jax.sharding import PartitionSpec as P

NEG = -1e30
LOG2E = math.log2(math.e)
TINY = 1e-30
FULL, SMALL, MATCH, GRADS = 60 << 20, 8 << 20, 48 << 20, 20 << 20


def dot(a, b):
    return jnp.dot(a, b, preferred_element_type=jnp.float32)


def dot_nt(a, b):
    return lax.dot_general(a, b, (((1,), (1,)), ((), ())), preferred_element_type=jnp.float32)


def pieces(x):
    high = x.astype(jnp.bfloat16)
    rest = x - high.astype(jnp.float32)
    mid = rest.astype(jnp.bfloat16)
    return high, mid, (rest - mid.astype(jnp.float32)).astype(jnp.bfloat16)


def exponent(x):
    return jnp.floor(jnp.log2(jnp.maximum(x, TINY)))


def block_kernel(keys, b_rows, log_decay, out):
    high, mid, low = pieces(log_decay[...])
    down = jnp.concatenate([high, mid, low, jnp.zeros((8, 128), jnp.bfloat16)], axis=0)
    key_cols, b_cols = keys[...].T, b_rows[...].T
    for k in range(out.shape[0]):
        out[k, 0:128] = key_cols
        out[k, 128:256] = b_cols
        out[k, 256:288] = down


def match_kernel(heads, scale2, group, place, own_b, other_b, q, c, c_cols, log_decay, weighted, own_grad, other_grad, loss,
                 scores, peak, total, fade, log_fade, key_fade, key_log, held, own_held, other_held, lost, sems):
    chip, core = place[0], place[1]
    chips, half = own_b.shape[0], q.shape[1]
    rows = heads * half
    full = chip // group

    u = lax.broadcasted_iota(jnp.int32, (128, 128), 0)
    v = lax.broadcasted_iota(jnp.int32, (128, 128), 1)
    after = jnp.where(u > v, 1.0, 0.0).astype(jnp.bfloat16)
    upto = jnp.where(u <= v, 1.0, 0.0).astype(jnp.bfloat16)
    lower = jnp.where(u >= v, 1.0, 0.0).astype(jnp.bfloat16)
    columns = jnp.concatenate([log_decay[...], jnp.zeros((128 - heads, 128), jnp.float32)], axis=0).T
    log_rows = sum(dot(lower, part) for part in pieces(columns)) * LOG2E
    for h in range(heads):
        row_log = jnp.broadcast_to(log_rows[:, h : h + 1], (half, 128))
        log_fade[h] = row_log
        fade[h] = jnp.exp2(row_log)
    def sums(ref, matrix):
        y = dot(ref[:, 256:288].reshape(chips * 32, 128), matrix).reshape(chips, 32, 128)
        return y[:, 0:8] + y[:, 8:16] + y[:, 16:24]

    ones = jnp.ones((128, 128), jnp.bfloat16)
    own_tail, other_tail = sums(own_b, after), sums(other_b, after)
    own_sum, other_sum = sums(own_b, ones), sums(other_b, ones)
    own_head = sums(own_b, upto)
    behind = jnp.zeros((8, 128), jnp.float32)
    for k in range(chips - 1, -1, -1):
        own = own_tail[k] + behind + jnp.where(core == 0, other_sum[k], 0.0)
        own = jnp.where(chip > k, own, -own_head[k]) * LOG2E
        other = behind + jnp.where(core == 0, 0.0, own_sum[k])
        other = (other_tail[k] + jnp.where(chip > k, other, 0.0)) * LOG2E
        for side, logs in enumerate((own, other)):
            key_log[2 * k + side] = logs
            key_fade[2 * k + side] = jnp.exp2(jnp.minimum(logs, 0.0))
        here = jnp.where(core == 0, 0.0, other_sum[k])
        behind = behind + jnp.where(chip > k, own_sum[k] + other_sum[k], jnp.where(chip == k, here, 0.0))

    def wide(x):
        return jnp.concatenate([x] * (2 * group), axis=1)

    def of_group(p, first):
        return jnp.concatenate(
            [ref[group * p + i, first : first + 128] for i in range(group) for ref in (own_b, other_b)], axis=1
        )

    def causal(p):
        apart = [2 * (group * p + i - chip) + side * (1 - 2 * core) for i in range(group) for side in range(2)]
        return jnp.concatenate([u - v >= 128 * x for x in apart], axis=1)

    peak[...] = jnp.full_like(peak, NEG)
    total[...] = jnp.zeros_like(total)

    def score(p, masked):
        s = dot(q[...].reshape(rows, 128), of_group(p, 0)) * scale2
        seen = causal(p) if masked else None
        for h in range(heads):
            at = slice(h * half, h * half + half)
            x = s[at]
            if masked:
                x = jnp.where(seen, x, NEG)
            scores[p, at] = x
            parts = [x[:, 128 * i : 128 * i + 128] for i in range(2 * group)]
            old = peak[h]
            top = functools.reduce(jnp.maximum, parts, old)
            total[h] = total[h] * jnp.exp2(old - top) + sum(jnp.exp2(y - top) for y in parts)
            peak[h] = top

    @pl.loop(0, full)
    def _(p):
        score(p, False)

    score(full, True)

    for h in range(heads):
        top = jnp.max(peak[h], axis=1, keepdims=True)
        summed = jnp.sum(total[h] * jnp.exp2(peak[h] - top), axis=1, keepdims=True)
        peak[h] = jnp.broadcast_to(top + jnp.log2(summed), (half, 128))
    lost[...] = jnp.zeros_like(lost)

    def copies(p):
        part = pl.ds(p * group, group)
        return (
            pltpu.make_async_copy(held.at[p], weighted.at[p], sems.at[0, p]),
            pltpu.make_async_copy(own_held.at[part], own_grad.at[part], sems.at[1, p]),
            pltpu.make_async_copy(other_held.at[part], other_grad.at[part], sems.at[2, p]),
        )

    @pl.loop(full + 1, chips // group)
    def _(p):
        for i in range(group):
            own_held[group * p + i] = jnp.zeros((128, 128), jnp.float32)
            other_held[group * p + i] = jnp.zeros((128, 128), jnp.float32)
        for x in copies(p)[1:]:
            x.start()

    def step(p, masked):
        kept = [2 * group * p + i for i in range(2 * group)]
        inner = dot(c[...].reshape(rows, 128), of_group(p, 128))
        seen = causal(p) if masked else None
        squares = jnp.zeros((8, 128), jnp.float32)
        for h in range(heads):
            at = slice(h * half, h * half + half)
            teacher = jnp.exp2(scores[p, at] - wide(peak[h]))
            if masked:
                logs = wide(log_fade[h]) + jnp.concatenate([key_log[k, h : h + 1] for k in kept], axis=1)
                decay = jnp.exp2(jnp.where(seen, logs, NEG))
            else:
                decay = wide(fade[h]) * jnp.concatenate([key_fade[k, h : h + 1] for k in kept], axis=1)
            mismatch = inner[at] * decay - teacher
            square = jnp.sum((mismatch * mismatch).reshape(half // 8, 8, 256 * group), axis=0)
            for i in range(2 * group):
                squares = squares + square[:, 128 * i : 128 * i + 128]
            held[p, at] = (mismatch * decay).astype(jnp.bfloat16)
        lost[...] += squares
        parts = dot(c_cols[...], held[p])
        for i in range(group):
            own_held[group * p + i] = parts[:, 256 * i : 256 * i + 128]
            other_held[group * p + i] = parts[:, 256 * i + 128 : 256 * i + 256]
        for x in copies(p):
            x.start()

    @pl.loop(0, full)
    def _(p):
        step(p, False)

    step(full, True)
    mean = jnp.broadcast_to(jnp.sum(lost[...], keepdims=True), (8, 128))
    for k in range(loss.shape[0]):
        loss[k] = mean

    @pl.loop(0, full + 1)
    def _(p):
        copies(p)[0].wait()

    @pl.loop(0, chips // group)
    def _(p):
        for x in copies(p)[1:]:
            x.wait()


def grad_kernel(group, place, own_b, other_b, weighted, grad_c, held, sems):
    full = place[0] // group

    def copy(p):
        return pltpu.make_async_copy(weighted.at[p], held.at[p], sems.at[p])

    @pl.loop(0, full + 1)
    def _(p):
        copy(p).start()

    grad_c[...] = jnp.zeros_like(grad_c)

    @pl.loop(0, full + 1)
    def _(p):
        copy(p).wait()
        b_cols = jnp.concatenate(
            [ref[group * p + i, 128:256] for i in range(group) for ref in (own_b, other_b)], axis=1
        )
        grad_c[...] += 2.0 * dot_nt(b_cols, held[p])


def scale_kernel(own, other, sent, power):
    blocks = own.shape[0]
    top = jnp.zeros((128, 128), jnp.float32)
    for k in range(blocks):
        x = own[k] + other[k]
        sent[k, 0:128] = x
        top = jnp.maximum(top, jnp.abs(x))
    level = exponent(jnp.broadcast_to(jnp.max(top, keepdims=True), (128, 128)))
    up = jnp.exp2(13.0 - level)
    for k in range(blocks):
        sent[k, 0:128] = sent[k, 0:128] * up
        sent[k, 128:144] = jnp.zeros((16, 128), jnp.float32)
    power[...] = level[0:8]


def extra_kernel(lost, power, extra):
    total = lost[0]
    for k in range(1, lost.shape[0]):
        total = total + lost[k]
    lost_power = exponent(total)
    share = total * jnp.exp2(-lost_power)
    coarse = jnp.floor(share * 1024.0) * (1.0 / 1024.0)
    lane = lax.broadcasted_iota(jnp.int32, (8, 128), 1)
    row = jnp.where(lane == 0, power[...], 0.0)
    row = jnp.where(lane == 1, lost_power, row)
    row = jnp.where(lane == 2, coarse, row)
    row = jnp.where(lane == 3, (share - coarse) * 1024.0, row)
    extra[...] = jnp.concatenate([row, row], axis=0)


def final_kernel(count, back, grad_b, mean):
    blocks = back.shape[0]
    total = jnp.zeros((128, 128), jnp.float32)
    loss = jnp.zeros((1, 128), jnp.float32)
    for k in range(blocks):
        extra = back[k, 128:129]
        power = jnp.broadcast_to(extra[:, 0:1], (1, 128))
        total = total + back[k, 0:128] * jnp.exp2(power - 13.0)
        share = extra[:, 2:3] + extra[:, 3:4] * (1.0 / 1024.0)
        loss = loss + jnp.broadcast_to(share * jnp.exp2(extra[:, 1:2]), (1, 128))
    grad_b[...] = 2.0 * total.T
    mean[...] = jnp.broadcast_to(loss * (1.0 / count), (8, 128))


def shards(queries, keys, c_proj, b_proj, log_decay):
    rows_dev, heads, size = queries.shape
    peers = lax.axis_size("context")
    z_size = lax.axis_size("head")
    chips = peers // 2
    rows = heads * rows_dev
    group = 4
    here = lax.axis_index("context")
    place = jnp.stack([here // 2, here % 2]).astype(jnp.int32)
    scale2 = LOG2E / math.sqrt(size)
    plane = [[2 * k + c for k in range(chips)] for c in range(2)]
    swap = [(i, i ^ 1) for i in range(peers)]

    f32 = functools.partial(jax.ShapeDtypeStruct, dtype=jnp.float32)
    bf16 = functools.partial(jax.ShapeDtypeStruct, dtype=jnp.bfloat16)
    smem = pl.BlockSpec(memory_space=pltpu.SMEM)
    vmem = pl.BlockSpec(memory_space=pltpu.VMEM)
    hbm = pl.BlockSpec(memory_space=pltpu.MemorySpace.HBM)
    work = rows * peers * 128
    steps = chips // group
    width = 256 * group

    down = log_decay.T
    block = pl.pallas_call(
        block_kernel,
        out_shape=bf16((chips, 288, 128)),
        in_specs=[vmem] * 3,
        out_specs=vmem,
        compiler_params=pltpu.CompilerParams(vmem_limit_bytes=FULL),
        name="block",
    )(keys[:, 0], b_proj[:, 0], down)
    own_b = lax.all_to_all(block, "context", 0, 0, axis_index_groups=plane)
    q, c = queries.transpose(1, 0, 2), c_proj.transpose(1, 0, 2)
    c_cols = c_proj.transpose(2, 1, 0).reshape(size, rows)
    own_b, q, c, c_cols, place = lax.optimization_barrier((own_b, q, c, c_cols, place))
    other_b = lax.ppermute(own_b, "context", swap)
    tile = pltpu.VMEM((heads, rows_dev, 128), jnp.float32)
    hbm_out = pltpu.MemorySpace.HBM
    weighted, own_sum, other_sum, lost = pl.pallas_call(
        functools.partial(match_kernel, heads, scale2, group),
        out_shape=(
            hbm_out((steps, rows, width), jnp.bfloat16),
            hbm_out((chips, size, 128), jnp.float32),
            hbm_out((chips, size, 128), jnp.float32),
            hbm_out((2 * z_size, 8, 128), jnp.float32),
        ),
        in_specs=[smem] + [vmem] * 6,
        out_specs=(hbm, hbm, hbm, pl.BlockSpec((2 * z_size, 8, 128), lambda: (0, 0, 0))),
        scratch_shapes=[pltpu.VMEM((steps, rows, width), jnp.float32)]
        + [tile] * 4
        + [pltpu.VMEM((peers, 8, 128), jnp.float32)] * 2
        + [pltpu.VMEM((steps, rows, width), jnp.bfloat16)]
        + [pltpu.VMEM((chips, size, 128), jnp.float32)] * 2
        + [pltpu.VMEM((8, 128), jnp.float32), pltpu.SemaphoreType.DMA((3, steps))],
        compiler_params=pltpu.CompilerParams(vmem_limit_bytes=MATCH),
        cost_estimate=pl.CostEstimate(flops=6 * work * size, bytes_accessed=12 << 20, transcendentals=3 * work),
        name="match",
    )(place, own_b, other_b, q, c, c_cols, down)

    columns = [[(2 * k + c) * z_size + z for c in range(2) for z in range(z_size)] for k in range(chips)]
    lost = lax.all_to_all(lost, ("context", "head"), 0, 0, axis_index_groups=columns)

    other_sum = lax.ppermute(other_sum, "context", swap)
    sent, power = pl.pallas_call(
        scale_kernel,
        out_shape=(f32((chips, 144, 128)), f32((8, 128))),
        in_specs=[vmem] * 2,
        out_specs=(vmem,) * 2,
        compiler_params=pltpu.CompilerParams(vmem_limit_bytes=SMALL),
        name="scale",
    )(own_sum, other_sum)
    sent, lost = lax.optimization_barrier((sent.astype(jnp.float16), lost))

    extra = pl.pallas_call(
        extra_kernel,
        out_shape=f32((16, 128)),
        in_specs=[vmem] * 2,
        out_specs=vmem,
        compiler_params=pltpu.CompilerParams(vmem_limit_bytes=SMALL),
        name="extra",
    )(lost, power)

    extra = jnp.broadcast_to(extra.astype(jnp.float16), (chips, 16, 128))
    sent = lax.dynamic_update_slice(sent, extra, (0, 128, 0))
    back = lax.all_to_all(sent, "context", 0, 0, axis_index_groups=plane)
    grad_c = pl.pallas_call(
        functools.partial(grad_kernel, group),
        out_shape=f32((size, rows)),
        in_specs=[smem, vmem, vmem, hbm],
        out_specs=vmem,
        scratch_shapes=[pltpu.VMEM((steps, rows, width), jnp.bfloat16), pltpu.SemaphoreType.DMA((steps,))],
        compiler_params=pltpu.CompilerParams(vmem_limit_bytes=GRADS),
        cost_estimate=pl.CostEstimate(flops=2 * work * size, bytes_accessed=10 << 20, transcendentals=0),
        name="grads",
    )(place, own_b, other_b, pltpu.with_memory_space_constraint(weighted, hbm_out))
    grad_c = grad_c.reshape(size, heads, rows_dev).transpose(2, 1, 0)
    mine, mean = pl.pallas_call(
        functools.partial(final_kernel, heads * z_size * peers * rows_dev),
        out_shape=(f32((rows_dev, size)), f32((8, 128))),
        in_specs=[vmem],
        out_specs=(vmem,) * 2,
        compiler_params=pltpu.CompilerParams(vmem_limit_bytes=SMALL),
        name="final",
    )(back.astype(jnp.float32))
    return mean[0, 0], grad_c, mine[:, None, :]


def solution(mesh):
    in_specs = (
        P("context", "head", None),
        P("context", "head", None),
        P("context", "head", None),
        P("context", "head", None),
        P("context", "head"),
    )
    out_specs = (P(), P("context", "head", None), P("context", "head", None))
    return jax.shard_map(shards, mesh=mesh, in_specs=in_specs, out_specs=out_specs, check_vma=False)
```

```python
import functools
import math

import jax
import jax.numpy as jnp
from jax import lax
from jax.experimental import pallas as pl
from jax.experimental.pallas import tpu as pltpu
from jax.sharding import PartitionSpec as P

NEG = -1e30
LOG2E = math.log2(math.e)
TINY = 1e-30
FULL, SMALL, MATCH = 60 << 20, 8 << 20, 40 << 20


def dot(a, b):
    return jnp.dot(a, b, preferred_element_type=jnp.float32)


def dot_nt(a, b):
    return lax.dot_general(a, b, (((1,), (1,)), ((), ())), preferred_element_type=jnp.float32)


def pieces(x):
    high = x.astype(jnp.bfloat16)
    rest = x - high.astype(jnp.float32)
    mid = rest.astype(jnp.bfloat16)
    return high, mid, (rest - mid.astype(jnp.float32)).astype(jnp.bfloat16)


def exponent(x):
    return jnp.floor(jnp.log2(jnp.maximum(x, TINY)))


def block_kernel(keys, b_rows, log_decay, out):
    high, mid, low = pieces(log_decay[...])
    down = jnp.concatenate([high, mid, low, jnp.zeros((8, 128), jnp.bfloat16)], axis=0)
    key_cols, b_cols = keys[...].T, b_rows[...].T
    for k in range(out.shape[0]):
        out[k, 0:128] = key_cols
        out[k, 128:256] = b_cols
        out[k, 256:288] = down


def match_kernel(scale2, group, place, own_b, other_b, own_qc, got_qc, own_sum, other_sum, keep, give, loss,
                 scores, peak, total, fade, log_fade, key_fade, key_log, sums_to, weighted, lost):
    chip, core, upper = place[0], place[1], place[2]
    chips, heads, half = own_b.shape[0], own_qc.shape[1], own_qc.shape[2]
    rows = heads * half
    q_c = (own_qc, got_qc)
    chip_of = (chip, chips - 1 - chip)
    core_of = (core, 1 - core)

    u = lax.broadcasted_iota(jnp.int32, (128, 128), 0)
    v = lax.broadcasted_iota(jnp.int32, (128, 128), 1)
    after = jnp.where(u > v, 1.0, 0.0).astype(jnp.bfloat16)
    upto = jnp.where(u <= v, 1.0, 0.0).astype(jnp.bfloat16)
    ones = jnp.ones((128, 128), jnp.bfloat16)

    def sums(ref, matrix):
        y = dot(ref[:, 256:288].reshape(chips * 32, 128), matrix).reshape(chips, 32, 128)
        y = (y[:, 0:8] + y[:, 8:16] + y[:, 16:24]) * LOG2E
        return jnp.where(upper == 0, y, jnp.concatenate([y[:, 4:8], y[:, 0:4]], axis=1))

    tails = sums(own_b, after), sums(other_b, after)
    whole = sums(own_b, ones), sums(other_b, ones)
    heads_of = sums(own_b, upto), sums(other_b, upto)
    low = jnp.where(core == 0, whole[0], whole[1])
    high = jnp.where(core == 0, whole[1], whole[0])
    for side in range(2):
        sums_to[side] = heads_of[side]
    for s in range(2):
        columns = jnp.concatenate([sums_to[s, chip_of[s]], jnp.zeros((120, 128), jnp.float32)], axis=0).T
        for h in range(heads):
            row_log = jnp.broadcast_to(columns[:, h : h + 1], (half, 128))
            log_fade[s, h] = row_log
            fade[s, h] = jnp.exp2(row_log)
        behind = jnp.zeros((8, 128), jnp.float32)
        for k in range(chips - 1, -1, -1):
            before, same = chip_of[s] > k, chip_of[s] == k
            for side in range(2):
                is_low = core == side
                more = behind + jnp.where(is_low, high[k], 0.0)
                logs = tails[side][k] + jnp.where(before, more, 0.0)
                if side == s:
                    logs = jnp.where(before, logs, -heads_of[side][k])
                key_log[s, 2 * k + side] = logs
                key_fade[s, 2 * k + side] = jnp.exp2(jnp.minimum(logs, 0.0))
            here = jnp.where(core_of[s] == 1, low[k], 0.0)
            behind = behind + jnp.where(before, low[k] + high[k], jnp.where(same, here, 0.0))

    def wide(x):
        return jnp.concatenate([x] * (2 * group), axis=1)

    def of_group(p, first):
        return jnp.concatenate(
            [ref[group * p + i, first : first + 128] for i in range(group) for ref in (own_b, other_b)], axis=1
        )

    def causal(s, p):
        other = (1 - 2 * core) * (1 - 2 * s)
        apart = [
            2 * (group * p + i - chip_of[s]) + (0 if side == s else other) for i in range(group) for side in range(2)
        ]
        return jnp.concatenate([u - v >= 128 * x for x in apart], axis=1)

    peak[...] = jnp.full_like(peak, NEG)
    total[...] = jnp.zeros_like(total)
    lost[...] = jnp.zeros_like(lost)
    keep[...] = jnp.zeros_like(keep)
    give[...] = jnp.zeros_like(give)
    own_sum[...] = jnp.zeros_like(own_sum)
    other_sum[...] = jnp.zeros_like(other_sum)

    def score(s, p, masked):
        x_all = dot(q_c[s][0].reshape(rows, 128), of_group(p, 0)) * scale2
        seen = causal(s, p) if masked else None
        for h in range(heads):
            at = slice(h * half, h * half + half)
            x = x_all[at]
            if masked:
                x = jnp.where(seen, x, NEG)
            scores[s, p, at] = x
            parts = [x[:, 128 * i : 128 * i + 128] for i in range(2 * group)]
            old = peak[s, h]
            top = functools.reduce(jnp.maximum, parts, old)
            total[s, h] = total[s, h] * jnp.exp2(old - top) + sum(jnp.exp2(y - top) for y in parts)
            peak[s, h] = top

    def step(s, p, masked):
        kept = [2 * group * p + i for i in range(2 * group)]
        b_cols = of_group(p, 128)
        inner = dot(q_c[s][1].reshape(rows, 128), b_cols)
        seen = causal(s, p) if masked else None
        squares = jnp.zeros((8, 128), jnp.float32)
        for h in range(heads):
            at = slice(h * half, h * half + half)
            teacher = jnp.exp2(scores[s, p, at] - wide(peak[s, h]))
            if masked:
                logs = wide(log_fade[s, h]) + jnp.concatenate([key_log[s, k, h : h + 1] for k in kept], axis=1)
                decay = jnp.exp2(jnp.where(seen, logs, NEG))
            else:
                decay = wide(fade[s, h]) * jnp.concatenate([key_fade[s, k, h : h + 1] for k in kept], axis=1)
            mismatch = inner[at] * decay - teacher
            square = jnp.sum((mismatch * mismatch).reshape(half // 8, 8, 256 * group), axis=0)
            for i in range(2 * group):
                squares = squares + square[:, 128 * i : 128 * i + 128]
            weighted[at] = (mismatch * decay).astype(jnp.bfloat16)
        lost[...] += squares
        c_cols = jnp.concatenate([q_c[s][1, h].T for h in range(heads)], axis=1)
        parts = dot(c_cols, weighted[...])
        for i in range(group):
            own_sum[group * p + i] += parts[:, 256 * i : 256 * i + 128]
            other_sum[group * p + i] += parts[:, 256 * i + 128 : 256 * i + 256]
        to = (keep, give)[s]
        to[...] += 2.0 * dot_nt(b_cols, weighted[...])

    for s in range(2):
        full = chip_of[s] // group

        @pl.loop(0, full)
        def _(p):
            score(s, p, False)

        score(s, full, True)

    for s in range(2):
        for h in range(heads):
            top = jnp.max(peak[s, h], axis=1, keepdims=True)
            summed = jnp.sum(total[s, h] * jnp.exp2(peak[s, h] - top), axis=1, keepdims=True)
            peak[s, h] = jnp.broadcast_to(top + jnp.log2(summed), (half, 128))

    for s in range(2):
        full = chip_of[s] // group

        @pl.loop(0, full)
        def _(p):
            step(s, p, False)

        step(s, full, True)

    loss[...] = jnp.broadcast_to(jnp.sum(lost[...], keepdims=True)[None], loss.shape)


def scale_kernel(own, other, sent, power):
    blocks = own.shape[0]
    top = jnp.zeros((128, 128), jnp.float32)
    for k in range(blocks):
        x = own[k] + other[k]
        sent[k, 0:128] = x
        top = jnp.maximum(top, jnp.abs(x))
    level = exponent(jnp.broadcast_to(jnp.max(top, keepdims=True), (128, 128)))
    up = jnp.exp2(13.0 - level)
    for k in range(blocks):
        sent[k, 0:128] = sent[k, 0:128] * up
        sent[k, 128:144] = jnp.zeros((16, 128), jnp.float32)
    power[...] = level[0:8]


def extra_kernel(lost, power, extra):
    total = jnp.broadcast_to(jnp.sum(lost[...], axis=0), (8, 128))
    lost_power = exponent(total)
    share = total * jnp.exp2(-lost_power)
    coarse = jnp.floor(share * 1024.0) * (1.0 / 1024.0)
    lane = lax.broadcasted_iota(jnp.int32, (8, 128), 1)
    row = jnp.where(lane == 0, power[...], 0.0)
    row = jnp.where(lane == 1, lost_power, row)
    row = jnp.where(lane == 2, coarse, row)
    row = jnp.where(lane == 3, (share - coarse) * 1024.0, row)
    extra[...] = jnp.concatenate([row, row], axis=0)


def final_kernel(count, back, grad_b, mean):
    blocks = back.shape[0]
    total = jnp.zeros((128, 128), jnp.float32)
    loss = jnp.zeros((1, 128), jnp.float32)
    for k in range(blocks):
        extra = back[k, 128:129]
        power = jnp.broadcast_to(extra[:, 0:1], (1, 128))
        total = total + back[k, 0:128] * jnp.exp2(power - 13.0)
        share = extra[:, 2:3] + extra[:, 3:4] * (1.0 / 1024.0)
        loss = loss + jnp.broadcast_to(share * jnp.exp2(extra[:, 1:2]), (1, 128))
    grad_b[...] = 2.0 * total.T
    mean[0, 0] = jnp.max(loss) * (1.0 / count)


def shards(queries, keys, c_proj, b_proj, log_decay):
    rows_dev, heads, size = queries.shape
    peers = lax.axis_size("context")
    z_size = lax.axis_size("head")
    chips = peers // 2
    rows = heads * rows_dev // 2
    group = 4
    here = lax.axis_index("context")
    upper = here // chips
    place = jnp.stack([here // 2, here % 2, upper]).astype(jnp.int32)
    scale2 = LOG2E / math.sqrt(size)
    plane = [[2 * k + c for k in range(chips)] for c in range(2)]
    swap = [(i, i ^ 1) for i in range(peers)]
    mirror = [(i, peers - 1 - i) for i in range(peers)]

    f32 = functools.partial(jax.ShapeDtypeStruct, dtype=jnp.float32)
    bf16 = functools.partial(jax.ShapeDtypeStruct, dtype=jnp.bfloat16)
    smem = pl.BlockSpec(memory_space=pltpu.SMEM)
    vmem = pl.BlockSpec(memory_space=pltpu.VMEM)
    work = rows * peers * 128
    steps = chips // group
    width = 256 * group

    down = log_decay.T
    block = pl.pallas_call(
        block_kernel,
        out_shape=bf16((chips, 288, 128)),
        in_specs=[vmem] * 3,
        out_specs=vmem,
        compiler_params=pltpu.CompilerParams(vmem_limit_bytes=FULL),
        name="block",
    )(keys[:, 0], b_proj[:, 0], down)
    own_b = lax.all_to_all(block, "context", 0, 0, axis_index_groups=plane)
    q_c = jnp.stack([queries, c_proj]).transpose(0, 2, 1, 3).reshape(2, 2, heads // 2, rows_dev, size)
    own_qc = jnp.where(upper == 0, q_c[:, 0], q_c[:, 1])
    got_qc = lax.ppermute(jnp.where(upper == 0, q_c[:, 1], q_c[:, 0]), "context", mirror)
    own_b, own_qc, got_qc, place = lax.optimization_barrier((own_b, own_qc, got_qc, place))
    other_b = lax.ppermute(own_b, "context", swap)

    tile = pltpu.VMEM((2, heads // 2, rows_dev, 128), jnp.float32)
    own_sum, other_sum, keep, give, lost = pl.pallas_call(
        functools.partial(match_kernel, scale2, group),
        out_shape=(f32((chips, size, 128)),) * 2
        + (f32((size, rows)),) * 2
        + (pltpu.MemorySpace.HBM((2 * z_size, 1, 128), jnp.float32),),
        in_specs=[smem] + [vmem] * 4,
        out_specs=(vmem,) * 4 + (pl.BlockSpec((2 * z_size, 1, 128), lambda: (0, 0, 0)),),
        scratch_shapes=[pltpu.VMEM((2, steps, rows, width), jnp.float32)]
        + [tile] * 4
        + [pltpu.VMEM((2, peers, 8, 128), jnp.float32)] * 2
        + [pltpu.VMEM((2, chips, 8, 128), jnp.float32), pltpu.VMEM((rows, width), jnp.bfloat16)]
        + [pltpu.VMEM((8, 128), jnp.float32)],
        compiler_params=pltpu.CompilerParams(vmem_limit_bytes=MATCH),
        cost_estimate=pl.CostEstimate(flops=6 * work * size, bytes_accessed=6 << 20, transcendentals=3 * work),
        name="match",
    )(place, own_b, other_b, own_qc, got_qc)

    columns = [[(2 * k + c) * z_size + z for c in range(2) for z in range(z_size)] for k in range(chips)]
    lost = lax.all_to_all(lost, ("context", "head"), 0, 0, axis_index_groups=columns)

    other_sum = lax.ppermute(other_sum, "context", swap)
    sent, power = pl.pallas_call(
        scale_kernel,
        out_shape=(f32((chips, 144, 128)), f32((8, 128))),
        in_specs=[vmem] * 2,
        out_specs=(vmem,) * 2,
        compiler_params=pltpu.CompilerParams(vmem_limit_bytes=SMALL),
        name="scale",
    )(own_sum, other_sum)
    sent, lost = lax.optimization_barrier((sent.astype(jnp.float16), lost))

    extra = pl.pallas_call(
        extra_kernel,
        out_shape=f32((16, 128)),
        in_specs=[vmem] * 2,
        out_specs=vmem,
        compiler_params=pltpu.CompilerParams(vmem_limit_bytes=SMALL),
        name="extra",
    )(lost, power)

    extra = jnp.broadcast_to(extra.astype(jnp.float16), (chips, 16, 128))
    sent = lax.dynamic_update_slice(sent, extra, (0, 128, 0))
    back = lax.all_to_all(sent, "context", 0, 0, axis_index_groups=plane)
    back_c = lax.ppermute(give, "context", mirror)
    grad_c = jnp.concatenate(
        [jnp.where(upper == 0, keep, back_c), jnp.where(upper == 0, back_c, keep)], axis=1
    )
    grad_c = grad_c.reshape(size, heads, rows_dev).transpose(2, 1, 0)
    mine, mean = pl.pallas_call(
        functools.partial(final_kernel, heads * z_size * peers * rows_dev),
        out_shape=(f32((rows_dev, size)), f32((1, 1))),
        in_specs=[vmem],
        out_specs=(vmem, smem),
        compiler_params=pltpu.CompilerParams(vmem_limit_bytes=SMALL),
        name="final",
    )(back.astype(jnp.float32))
    return mean[0, 0], grad_c, mine[:, None, :]


def solution(mesh):
    in_specs = (
        P("context", "head", None),
        P("context", "head", None),
        P("context", "head", None),
        P("context", "head", None),
        P("context", "head"),
    )
    out_specs = (P(), P("context", "head", None), P("context", "head", None))
    return jax.shard_map(shards, mesh=mesh, in_specs=in_specs, out_specs=out_specs, check_vma=False)
```

```python
import functools
import math

import jax
import jax.numpy as jnp
from jax import lax
from jax.experimental import pallas as pl
from jax.experimental.pallas import tpu as pltpu
from jax.sharding import PartitionSpec as P

NEG = -1e30
LOG2E = math.log2(math.e)
TINY = 1e-30
FULL, SMALL, MATCH, GRADS = 60 << 20, 8 << 20, 48 << 20, 20 << 20


def dot(a, b):
    return jnp.dot(a, b, preferred_element_type=jnp.float32)


def dot_nt(a, b):
    return lax.dot_general(a, b, (((1,), (1,)), ((), ())), preferred_element_type=jnp.float32)


def pieces(x):
    high = x.astype(jnp.bfloat16)
    rest = x - high.astype(jnp.float32)
    mid = rest.astype(jnp.bfloat16)
    return high, mid, (rest - mid.astype(jnp.float32)).astype(jnp.bfloat16)


def exponent(x):
    return jnp.floor(jnp.log2(jnp.maximum(x, TINY)))


def block_kernel(keys_from, b_from, log_from, out, keys, b_rows, log_decay, sems):
    copies = [
        pltpu.make_async_copy(x, y, sems.at[i])
        for i, (x, y) in enumerate(((keys_from, keys), (b_from, b_rows), (log_from, log_decay)))
    ]
    for x in copies:
        x.start()
    for x in copies:
        x.wait()
    high, mid, low = pieces(log_decay[...])
    down = jnp.concatenate([high, mid, low, jnp.zeros((8, 128), jnp.bfloat16)], axis=0)
    key_cols, b_cols = keys[...].T, b_rows[...].T
    for k in range(out.shape[0]):
        out[k, 0:128] = key_cols
        out[k, 128:256] = b_cols
        out[k, 256:288] = down


def match_kernel(heads, scale2, group, place, own_b, other_b, q, c, c_cols, log_decay, weighted, own_grad, other_grad, loss,
                 scores, tops, peak, total, fade, log_fade, key_fade, key_log, held, own_held, other_held, lost, sems):
    chip, core = place[0], place[1]
    chips, half = own_b.shape[0], q.shape[1]
    rows = heads * half
    full = chip // group

    u = lax.broadcasted_iota(jnp.int32, (128, 128), 0)
    v = lax.broadcasted_iota(jnp.int32, (128, 128), 1)
    after = jnp.where(u > v, 1.0, 0.0).astype(jnp.bfloat16)
    upto = jnp.where(u <= v, 1.0, 0.0).astype(jnp.bfloat16)
    lower = jnp.where(u >= v, 1.0, 0.0).astype(jnp.bfloat16)
    columns = jnp.concatenate([log_decay[...], jnp.zeros((128 - heads, 128), jnp.float32)], axis=0).T
    log_rows = sum(dot(lower, part) for part in pieces(columns)) * LOG2E
    for h in range(heads):
        row_log = jnp.broadcast_to(log_rows[:, h : h + 1], (half, 128))
        log_fade[h] = row_log
        fade[h] = jnp.exp2(row_log)
    def sums(ref, matrix):
        y = dot(ref[:, 256:288].reshape(chips * 32, 128), matrix).reshape(chips, 32, 128)
        return y[:, 0:8] + y[:, 8:16] + y[:, 16:24]

    ones = jnp.ones((128, 128), jnp.bfloat16)
    own_tail, other_tail = sums(own_b, after), sums(other_b, after)
    own_sum, other_sum = sums(own_b, ones), sums(other_b, ones)
    own_head = sums(own_b, upto)
    behind = jnp.zeros((8, 128), jnp.float32)
    for k in range(chips - 1, -1, -1):
        own = own_tail[k] + behind + jnp.where(core == 0, other_sum[k], 0.0)
        own = jnp.where(chip > k, own, -own_head[k]) * LOG2E
        other = behind + jnp.where(core == 0, 0.0, own_sum[k])
        other = (other_tail[k] + jnp.where(chip > k, other, 0.0)) * LOG2E
        for side, logs in enumerate((own, other)):
            key_log[2 * k + side] = logs
            key_fade[2 * k + side] = jnp.exp2(jnp.minimum(logs, 0.0))
        here = jnp.where(core == 0, 0.0, other_sum[k])
        behind = behind + jnp.where(chip > k, own_sum[k] + other_sum[k], jnp.where(chip == k, here, 0.0))

    def wide(x):
        return jnp.concatenate([x] * (2 * group), axis=1)

    def of_group(p, first):
        return jnp.concatenate(
            [ref[group * p + i, first : first + 128] for i in range(group) for ref in (own_b, other_b)], axis=1
        )

    def causal(p):
        apart = [2 * (group * p + i - chip) + side * (1 - 2 * core) for i in range(group) for side in range(2)]
        return jnp.concatenate([u - v >= 128 * x for x in apart], axis=1)

    peak[...] = jnp.full_like(peak, NEG)
    total[...] = jnp.zeros_like(total)

    def score(p, masked):
        s = dot(q[...].reshape(rows, 128), of_group(p, 0)) * scale2
        seen = causal(p) if masked else None
        for h in range(heads):
            at = slice(h * half, h * half + half)
            x = s[at]
            if masked:
                x = jnp.where(seen, x, NEG)
            parts = [x[:, 128 * i : 128 * i + 128] for i in range(2 * group)]
            old = peak[h]
            top = functools.reduce(jnp.maximum, parts, old)
            grown = [jnp.exp2(y - top) for y in parts]
            for i in range(2 * group):
                scores[p, at, 128 * i : 128 * i + 128] = grown[i]
            total[h] = total[h] * jnp.exp2(old - top) + sum(grown)
            peak[h] = top
            tops[p, h] = top

    @pl.loop(0, full)
    def _(p):
        score(p, False)

    score(full, True)

    for h in range(heads):
        top = jnp.max(peak[h], axis=1, keepdims=True)
        summed = jnp.sum(total[h] * jnp.exp2(peak[h] - top), axis=1, keepdims=True)
        peak[h] = jnp.broadcast_to(top + jnp.log2(summed), (half, 128))
    lost[...] = jnp.zeros_like(lost)

    def copies(p):
        part = pl.ds(p * group, group)
        return (
            pltpu.make_async_copy(own_held.at[part], own_grad.at[part], sems.at[heads, p]),
            pltpu.make_async_copy(other_held.at[part], other_grad.at[part], sems.at[heads + 1, p]),
        )

    def copy(p, h):
        at = pl.ds(h * half, half)
        return pltpu.make_async_copy(held.at[p, at], weighted.at[p, at], sems.at[h, p])

    @pl.loop(full + 1, chips // group)
    def _(p):
        for i in range(group):
            own_held[group * p + i] = jnp.zeros((128, 128), jnp.float32)
            other_held[group * p + i] = jnp.zeros((128, 128), jnp.float32)
        for x in copies(p):
            x.start()

    def step(p, masked):
        kept = [2 * group * p + i for i in range(2 * group)]
        inner = dot(c[...].reshape(rows, 128), of_group(p, 128))
        seen = causal(p) if masked else None
        squares = jnp.zeros((8, 128), jnp.float32)
        for h in range(heads):
            at = slice(h * half, h * half + half)
            teacher = scores[p, at] * wide(jnp.exp2(tops[p, h] - peak[h]))
            if masked:
                logs = wide(log_fade[h]) + jnp.concatenate([key_log[k, h : h + 1] for k in kept], axis=1)
                decay = jnp.exp2(jnp.where(seen, logs, NEG))
            else:
                decay = wide(fade[h]) * jnp.concatenate([key_fade[k, h : h + 1] for k in kept], axis=1)
            mismatch = inner[at] * decay - teacher
            square = jnp.sum((mismatch * mismatch).reshape(half // 8, 8, 256 * group), axis=0)
            for i in range(2 * group):
                squares = squares + square[:, 128 * i : 128 * i + 128]
            held[p, at] = (mismatch * decay).astype(jnp.bfloat16)
            copy(p, h).start()
        lost[...] += squares
        parts = dot(c_cols[...], held[p])
        for i in range(group):
            own_held[group * p + i] = parts[:, 256 * i : 256 * i + 128]
            other_held[group * p + i] = parts[:, 256 * i + 128 : 256 * i + 256]
        for x in copies(p):
            x.start()

    @pl.loop(0, full)
    def _(p):
        step(p, False)

    step(full, True)
    loss[...] = jnp.broadcast_to(jnp.sum(lost[...], keepdims=True)[None], loss.shape)

    @pl.loop(0, full + 1)
    def _(p):
        for h in range(heads):
            copy(p, h).wait()

    @pl.loop(0, chips // group)
    def _(p):
        for x in copies(p):
            x.wait()


def grad_kernel(group, place, own_b, other_b, weighted, grad_c, held, sems):
    full = place[0] // group

    def copy(p):
        return pltpu.make_async_copy(weighted.at[p], held.at[p], sems.at[p])

    @pl.loop(0, full + 1)
    def _(p):
        copy(p).start()

    grad_c[...] = jnp.zeros_like(grad_c)

    @pl.loop(0, full + 1)
    def _(p):
        copy(p).wait()
        b_cols = jnp.concatenate(
            [ref[group * p + i, 128:256] for i in range(group) for ref in (own_b, other_b)], axis=1
        )
        grad_c[...] += 2.0 * dot_nt(b_cols, held[p])


def scale_kernel(own, other, sent, power):
    blocks = own.shape[0]
    top = jnp.zeros((128, 128), jnp.float32)
    for k in range(blocks):
        x = own[k] + other[k]
        sent[k, 0:128] = x
        top = jnp.maximum(top, jnp.abs(x))
    level = exponent(jnp.broadcast_to(jnp.max(top, keepdims=True), (128, 128)))
    up = jnp.exp2(13.0 - level)
    for k in range(blocks):
        sent[k, 0:128] = sent[k, 0:128] * up
        sent[k, 128:144] = jnp.zeros((16, 128), jnp.float32)
    power[...] = level[0:8]


def extra_kernel(lost, power, extra):
    total = jnp.broadcast_to(jnp.sum(lost[...], axis=0), (8, 128))
    lost_power = exponent(total)
    share = total * jnp.exp2(-lost_power)
    coarse = jnp.floor(share * 1024.0) * (1.0 / 1024.0)
    lane = lax.broadcasted_iota(jnp.int32, (8, 128), 1)
    row = jnp.where(lane == 0, power[...], 0.0)
    row = jnp.where(lane == 1, lost_power, row)
    row = jnp.where(lane == 2, coarse, row)
    row = jnp.where(lane == 3, (share - coarse) * 1024.0, row)
    extra[...] = jnp.concatenate([row, row], axis=0)


def final_kernel(count, back, grad_b, mean):
    blocks = back.shape[0]
    total = jnp.zeros((128, 128), jnp.float32)
    loss = jnp.zeros((1, 128), jnp.float32)
    for k in range(blocks):
        extra = back[k, 128:129]
        power = jnp.broadcast_to(extra[:, 0:1], (1, 128))
        total = total + back[k, 0:128] * jnp.exp2(power - 13.0)
        share = extra[:, 2:3] + extra[:, 3:4] * (1.0 / 1024.0)
        loss = loss + jnp.broadcast_to(share * jnp.exp2(extra[:, 1:2]), (1, 128))
    grad_b[...] = 2.0 * total.T
    mean[0, 0] = jnp.max(loss) * (1.0 / count)


def shards(queries, keys, c_proj, b_proj, log_decay):
    rows_dev, heads, size = queries.shape
    peers = lax.axis_size("context")
    z_size = lax.axis_size("head")
    chips = peers // 2
    rows = heads * rows_dev
    group = 4
    here = lax.axis_index("context")
    place = jnp.stack([here // 2, here % 2]).astype(jnp.int32)
    scale2 = LOG2E / math.sqrt(size)
    plane = [[2 * k + c for k in range(chips)] for c in range(2)]
    swap = [(i, i ^ 1) for i in range(peers)]

    f32 = functools.partial(jax.ShapeDtypeStruct, dtype=jnp.float32)
    bf16 = functools.partial(jax.ShapeDtypeStruct, dtype=jnp.bfloat16)
    smem = pl.BlockSpec(memory_space=pltpu.SMEM)
    vmem = pl.BlockSpec(memory_space=pltpu.VMEM)
    hbm_out = pltpu.MemorySpace.HBM
    hbm = pl.BlockSpec(memory_space=hbm_out)
    work = rows * peers * 128
    steps = chips // group
    width = 256 * group

    down = log_decay.T
    block = pl.pallas_call(
        block_kernel,
        out_shape=bf16((chips, 288, 128)),
        in_specs=[hbm] * 3,
        out_specs=vmem,
        scratch_shapes=[pltpu.VMEM((rows_dev, size), jnp.bfloat16)] * 2
        + [pltpu.VMEM((heads, rows_dev), jnp.float32), pltpu.SemaphoreType.DMA((3,))],
        compiler_params=pltpu.CompilerParams(vmem_limit_bytes=SMALL),
        name="block",
    )(*(pltpu.with_memory_space_constraint(x, hbm_out) for x in (keys[:, 0], b_proj[:, 0], down)))
    own_b = lax.all_to_all(block, "context", 0, 0, axis_index_groups=plane)
    q, c = queries.transpose(1, 0, 2), c_proj.transpose(1, 0, 2)
    c_cols = c_proj.transpose(2, 1, 0).reshape(size, rows)
    own_b, q, c, c_cols, place = lax.optimization_barrier((own_b, q, c, c_cols, place))
    other_b = lax.ppermute(own_b, "context", swap)
    tile = pltpu.VMEM((heads, rows_dev, 128), jnp.float32)
    weighted, own_sum, other_sum, lost = pl.pallas_call(
        functools.partial(match_kernel, heads, scale2, group),
        out_shape=(
            hbm_out((steps, rows, width), jnp.bfloat16),
            hbm_out((chips, size, 128), jnp.float32),
            hbm_out((chips, size, 128), jnp.float32),
            hbm_out((2 * z_size, 1, 128), jnp.float32),
        ),
        in_specs=[smem] + [vmem] * 6,
        out_specs=(hbm, hbm, hbm, pl.BlockSpec((2 * z_size, 1, 128), lambda: (0, 0, 0))),
        scratch_shapes=[pltpu.VMEM((steps, rows, width), jnp.float32)]
        + [pltpu.VMEM((steps, heads, rows_dev, 128), jnp.float32)]
        + [tile] * 4
        + [pltpu.VMEM((peers, 8, 128), jnp.float32)] * 2
        + [pltpu.VMEM((steps, rows, width), jnp.bfloat16)]
        + [pltpu.VMEM((chips, size, 128), jnp.float32)] * 2
        + [pltpu.VMEM((8, 128), jnp.float32), pltpu.SemaphoreType.DMA((heads + 2, steps))],
        compiler_params=pltpu.CompilerParams(vmem_limit_bytes=MATCH),
        cost_estimate=pl.CostEstimate(flops=6 * work * size, bytes_accessed=12 << 20, transcendentals=3 * work),
        name="match",
    )(place, own_b, other_b, q, c, c_cols, down)

    columns = [[(2 * k + c) * z_size + z for c in range(2) for z in range(z_size)] for k in range(chips)]
    lost = lax.all_to_all(lost, ("context", "head"), 0, 0, axis_index_groups=columns)

    other_sum = lax.ppermute(other_sum, "context", swap)
    sent, power = pl.pallas_call(
        scale_kernel,
        out_shape=(f32((chips, 144, 128)), f32((8, 128))),
        in_specs=[vmem] * 2,
        out_specs=(vmem,) * 2,
        compiler_params=pltpu.CompilerParams(vmem_limit_bytes=SMALL),
        name="scale",
    )(own_sum, other_sum)
    sent, lost = lax.optimization_barrier((sent.astype(jnp.float16), lost))

    extra = pl.pallas_call(
        extra_kernel,
        out_shape=f32((16, 128)),
        in_specs=[vmem] * 2,
        out_specs=vmem,
        compiler_params=pltpu.CompilerParams(vmem_limit_bytes=SMALL),
        name="extra",
    )(lost, power)

    extra = jnp.broadcast_to(extra.astype(jnp.float16), (chips, 16, 128))
    sent = lax.dynamic_update_slice(sent, extra, (0, 128, 0))
    back = lax.all_to_all(sent, "context", 0, 0, axis_index_groups=plane)
    grad_c = pl.pallas_call(
        functools.partial(grad_kernel, group),
        out_shape=f32((size, rows)),
        in_specs=[smem, vmem, vmem, hbm],
        out_specs=vmem,
        scratch_shapes=[pltpu.VMEM((steps, rows, width), jnp.bfloat16), pltpu.SemaphoreType.DMA((steps,))],
        compiler_params=pltpu.CompilerParams(vmem_limit_bytes=GRADS),
        cost_estimate=pl.CostEstimate(flops=2 * work * size, bytes_accessed=10 << 20, transcendentals=0),
        name="grads",
    )(place, own_b, other_b, pltpu.with_memory_space_constraint(weighted, hbm_out))
    grad_c = grad_c.reshape(size, heads, rows_dev).transpose(2, 1, 0)
    mine, mean = pl.pallas_call(
        functools.partial(final_kernel, heads * z_size * peers * rows_dev),
        out_shape=(f32((rows_dev, size)), f32((1, 1))),
        in_specs=[vmem],
        out_specs=(vmem, smem),
        compiler_params=pltpu.CompilerParams(vmem_limit_bytes=SMALL),
        name="final",
    )(back.astype(jnp.float32))
    return mean[0, 0], grad_c, mine[:, None, :]


def solution(mesh):
    in_specs = (
        P("context", "head", None),
        P("context", "head", None),
        P("context", "head", None),
        P("context", "head", None),
        P("context", "head"),
    )
    out_specs = (P(), P("context", "head", None), P("context", "head", None))
    return jax.shard_map(shards, mesh=mesh, in_specs=in_specs, out_specs=out_specs, check_vma=False)
```

```python
import functools
import math

import jax
import jax.numpy as jnp
from jax import lax
from jax.experimental import pallas as pl
from jax.experimental.pallas import tpu as pltpu
from jax.sharding import PartitionSpec as P

NEG = -1e30
LOG2E = math.log2(math.e)
TINY = 1e-30
FULL, SMALL, MATCH, GRADS = 60 << 20, 8 << 20, 48 << 20, 20 << 20


def dot(a, b):
    return jnp.dot(a, b, preferred_element_type=jnp.float32)


def dot_nt(a, b):
    return lax.dot_general(a, b, (((1,), (1,)), ((), ())), preferred_element_type=jnp.float32)


def pieces(x):
    high = x.astype(jnp.bfloat16)
    rest = x - high.astype(jnp.float32)
    mid = rest.astype(jnp.bfloat16)
    return high, mid, (rest - mid.astype(jnp.float32)).astype(jnp.bfloat16)


def exponent(x):
    return jnp.floor(jnp.log2(jnp.maximum(x, TINY)))


def block_kernel(keys_from, b_from, log_from, out, keys, b_rows, log_decay, block, sems):
    copies = [
        pltpu.make_async_copy(x, y, sems.at[i])
        for i, (x, y) in enumerate(((keys_from, keys), (b_from, b_rows), (log_from, log_decay)))
    ]
    for x in copies:
        x.start()
    for x in copies:
        x.wait()
    block[0:128] = keys[...].T
    block[128:256] = b_rows[...].T
    block[256:272] = jnp.concatenate(pieces(log_decay[...])[:2], axis=0)
    copies = [pltpu.make_async_copy(block, out.at[k], sems.at[3 + k]) for k in range(out.shape[0])]
    for x in copies:
        x.start()
    for x in copies:
        x.wait()


def match_kernel(heads, scale2, group, place, own_b, other_b, q, c, c_cols, log_decay, weighted, own_grad, other_grad, loss,
                 scores, tops, peak, total, fade, log_fade, key_fade, key_log, held, own_held, other_held, lost, sems):
    chip, core = place[0], place[1]
    chips, half = own_b.shape[0], q.shape[1]
    rows = heads * half
    full = chip // group

    u = lax.broadcasted_iota(jnp.int32, (128, 128), 0)
    v = lax.broadcasted_iota(jnp.int32, (128, 128), 1)
    after = jnp.where(u > v, 1.0, 0.0).astype(jnp.bfloat16)
    upto = jnp.where(u <= v, 1.0, 0.0).astype(jnp.bfloat16)
    lower = jnp.where(u >= v, 1.0, 0.0).astype(jnp.bfloat16)
    columns = jnp.concatenate([log_decay[...], jnp.zeros((128 - heads, 128), jnp.float32)], axis=0).T
    log_rows = sum(dot(lower, part) for part in pieces(columns)[:2]) * LOG2E
    for h in range(heads):
        row_log = jnp.broadcast_to(log_rows[:, h : h + 1], (half, 128))
        log_fade[h] = row_log
        fade[h] = jnp.exp2(row_log)
    def sums(ref, matrix):
        y = dot(ref[:, 256:272].reshape(chips * 16, 128), matrix).reshape(chips, 16, 128)
        return y[:, 0:8] + y[:, 8:16]

    ones = jnp.ones((128, 128), jnp.bfloat16)
    own_tail, other_tail = sums(own_b, after), sums(other_b, after)
    own_sum, other_sum = sums(own_b, ones), sums(other_b, ones)
    own_head = sums(own_b, upto)
    behind = jnp.zeros((8, 128), jnp.float32)
    for k in range(chips - 1, -1, -1):
        own = own_tail[k] + behind + jnp.where(core == 0, other_sum[k], 0.0)
        own = jnp.where(chip > k, own, -own_head[k]) * LOG2E
        other = behind + jnp.where(core == 0, 0.0, own_sum[k])
        other = (other_tail[k] + jnp.where(chip > k, other, 0.0)) * LOG2E
        for side, logs in enumerate((own, other)):
            key_log[2 * k + side] = logs
            key_fade[2 * k + side] = jnp.exp2(jnp.minimum(logs, 0.0))
        here = jnp.where(core == 0, 0.0, other_sum[k])
        behind = behind + jnp.where(chip > k, own_sum[k] + other_sum[k], jnp.where(chip == k, here, 0.0))

    def wide(x):
        return jnp.concatenate([x] * (2 * group), axis=1)

    def of_group(p, first):
        return jnp.concatenate(
            [ref[group * p + i, first : first + 128] for i in range(group) for ref in (own_b, other_b)], axis=1
        )

    def causal(p):
        apart = [2 * (group * p + i - chip) + side * (1 - 2 * core) for i in range(group) for side in range(2)]
        return jnp.concatenate([u - v >= 128 * x for x in apart], axis=1)

    peak[...] = jnp.full_like(peak, NEG)
    total[...] = jnp.zeros_like(total)

    def score(p, masked):
        s = dot(q[...].reshape(rows, 128), of_group(p, 0)) * scale2
        seen = causal(p) if masked else None
        for h in range(heads):
            at = slice(h * half, h * half + half)
            x = s[at]
            if masked:
                x = jnp.where(seen, x, NEG)
            parts = [x[:, 128 * i : 128 * i + 128] for i in range(2 * group)]
            old = peak[h]
            top = functools.reduce(jnp.maximum, parts, old)
            grown = [jnp.exp2(y - top) for y in parts]
            for i in range(2 * group):
                scores[p, at, 128 * i : 128 * i + 128] = grown[i]
            total[h] = total[h] * jnp.exp2(old - top) + sum(grown)
            peak[h] = top
            tops[p, h] = top

    @pl.loop(0, full)
    def _(p):
        score(p, False)

    score(full, True)

    for h in range(heads):
        top = jnp.max(peak[h], axis=1, keepdims=True)
        summed = jnp.sum(total[h] * jnp.exp2(peak[h] - top), axis=1, keepdims=True)
        peak[h] = jnp.broadcast_to(top + jnp.log2(summed), (half, 128))
    lost[...] = jnp.zeros_like(lost)

    def copies(p):
        part = pl.ds(p * group, group)
        return (
            pltpu.make_async_copy(own_held.at[part], own_grad.at[part], sems.at[heads, p]),
            pltpu.make_async_copy(other_held.at[part], other_grad.at[part], sems.at[heads + 1, p]),
        )

    def copy(p, h):
        at = pl.ds(h * half, half)
        return pltpu.make_async_copy(held.at[p, at], weighted.at[p, at], sems.at[h, p])

    @pl.loop(full + 1, chips // group)
    def _(p):
        for i in range(group):
            own_held[group * p + i] = jnp.zeros((128, 128), jnp.float32)
            other_held[group * p + i] = jnp.zeros((128, 128), jnp.float32)
        for x in copies(p):
            x.start()

    def step(p, masked):
        kept = [2 * group * p + i for i in range(2 * group)]
        inner = dot(c[...].reshape(rows, 128), of_group(p, 128))
        seen = causal(p) if masked else None
        squares = jnp.zeros((8, 128), jnp.float32)
        for h in range(heads):
            at = slice(h * half, h * half + half)
            teacher = scores[p, at] * wide(jnp.exp2(tops[p, h] - peak[h]))
            if masked:
                logs = wide(log_fade[h]) + jnp.concatenate([key_log[k, h : h + 1] for k in kept], axis=1)
                decay = jnp.exp2(jnp.where(seen, logs, NEG))
            else:
                decay = wide(fade[h]) * jnp.concatenate([key_fade[k, h : h + 1] for k in kept], axis=1)
            mismatch = inner[at] * decay - teacher
            square = jnp.sum((mismatch * mismatch).reshape(half // 8, 8, 256 * group), axis=0)
            for i in range(2 * group):
                squares = squares + square[:, 128 * i : 128 * i + 128]
            held[p, at] = (mismatch * decay).astype(jnp.bfloat16)
            copy(p, h).start()
        lost[...] += squares
        parts = dot(c_cols[...], held[p])
        for i in range(group):
            own_held[group * p + i] = parts[:, 256 * i : 256 * i + 128]
            other_held[group * p + i] = parts[:, 256 * i + 128 : 256 * i + 256]
        for x in copies(p):
            x.start()

    @pl.loop(0, full)
    def _(p):
        step(p, False)

    step(full, True)
    loss[...] = jnp.broadcast_to(jnp.sum(lost[...], keepdims=True)[None], loss.shape)

    @pl.loop(0, full + 1)
    def _(p):
        for h in range(heads):
            copy(p, h).wait()

    @pl.loop(0, chips // group)
    def _(p):
        for x in copies(p):
            x.wait()


def grad_kernel(group, place, own_b, other_b, weighted, grad_c, held, sems):
    full = place[0] // group

    def copy(p):
        return pltpu.make_async_copy(weighted.at[p], held.at[p], sems.at[p])

    @pl.loop(0, full + 1)
    def _(p):
        copy(p).start()

    grad_c[...] = jnp.zeros_like(grad_c)

    @pl.loop(0, full + 1)
    def _(p):
        copy(p).wait()
        b_cols = jnp.concatenate(
            [ref[group * p + i, 128:256] for i in range(group) for ref in (own_b, other_b)], axis=1
        )
        grad_c[...] += 2.0 * dot_nt(b_cols, held[p])


def scale_kernel(own, other, sent, power):
    blocks = own.shape[0]
    top = jnp.zeros((128, 128), jnp.float32)
    for k in range(blocks):
        x = own[k] + other[k]
        sent[k, 0:128] = x
        top = jnp.maximum(top, jnp.abs(x))
    level = exponent(jnp.broadcast_to(jnp.max(top, keepdims=True), (128, 128)))
    up = jnp.exp2(13.0 - level)
    for k in range(blocks):
        sent[k, 0:128] = sent[k, 0:128] * up
        sent[k, 128:136] = jnp.zeros((8, 128), jnp.float32)
    power[...] = level[0:8]


def extra_kernel(lost, power, extra):
    total = jnp.broadcast_to(jnp.sum(lost[...], axis=0), (8, 128))
    lost_power = exponent(total)
    share = total * jnp.exp2(-lost_power)
    coarse = jnp.floor(share * 1024.0) * (1.0 / 1024.0)
    lane = lax.broadcasted_iota(jnp.int32, (8, 128), 1)
    row = jnp.where(lane == 0, power[...], 0.0)
    row = jnp.where(lane == 1, lost_power, row)
    row = jnp.where(lane == 2, coarse, row)
    row = jnp.where(lane == 3, (share - coarse) * 1024.0, row)
    extra[...] = row


def final_kernel(count, back, grad_b, mean):
    blocks = back.shape[0]
    total = jnp.zeros((128, 128), jnp.float32)
    loss = jnp.zeros((1, 128), jnp.float32)
    for k in range(blocks):
        extra = back[k, 128:129]
        power = jnp.broadcast_to(extra[:, 0:1], (1, 128))
        total = total + back[k, 0:128] * jnp.exp2(power - 13.0)
        share = extra[:, 2:3] + extra[:, 3:4] * (1.0 / 1024.0)
        loss = loss + jnp.broadcast_to(share * jnp.exp2(extra[:, 1:2]), (1, 128))
    grad_b[...] = 2.0 * total.T
    mean[0, 0] = jnp.max(loss) * (1.0 / count)


def shards(queries, keys, c_proj, b_proj, log_decay):
    rows_dev, heads, size = queries.shape
    peers = lax.axis_size("context")
    z_size = lax.axis_size("head")
    chips = peers // 2
    rows = heads * rows_dev
    group = 4
    here = lax.axis_index("context")
    place = jnp.stack([here // 2, here % 2]).astype(jnp.int32)
    scale2 = LOG2E / math.sqrt(size)
    plane = [[2 * k + c for k in range(chips)] for c in range(2)]
    swap = [(i, i ^ 1) for i in range(peers)]

    f32 = functools.partial(jax.ShapeDtypeStruct, dtype=jnp.float32)
    bf16 = functools.partial(jax.ShapeDtypeStruct, dtype=jnp.bfloat16)
    smem = pl.BlockSpec(memory_space=pltpu.SMEM)
    vmem = pl.BlockSpec(memory_space=pltpu.VMEM)
    hbm_out = pltpu.MemorySpace.HBM
    hbm = pl.BlockSpec(memory_space=hbm_out)
    work = rows * peers * 128
    steps = chips // group
    width = 256 * group

    down = log_decay.T
    block = pl.pallas_call(
        block_kernel,
        out_shape=hbm_out((chips, 272, 128), jnp.bfloat16),
        in_specs=[hbm] * 3,
        out_specs=hbm,
        scratch_shapes=[pltpu.VMEM((rows_dev, size), jnp.bfloat16)] * 2
        + [pltpu.VMEM((heads, rows_dev), jnp.float32), pltpu.VMEM((272, 128), jnp.bfloat16)]
        + [pltpu.SemaphoreType.DMA((3 + chips,))],
        compiler_params=pltpu.CompilerParams(vmem_limit_bytes=SMALL),
        name="block",
    )(*(pltpu.with_memory_space_constraint(x, hbm_out) for x in (keys[:, 0], b_proj[:, 0], down)))
    own_b = lax.all_to_all(block, "context", 0, 0, axis_index_groups=plane)
    q, c = queries.transpose(1, 0, 2), c_proj.transpose(1, 0, 2)
    c_cols = c_proj.transpose(2, 1, 0).reshape(size, rows)
    own_b, q, c, c_cols, place = lax.optimization_barrier((own_b, q, c, c_cols, place))
    other_b = lax.ppermute(own_b, "context", swap)
    tile = pltpu.VMEM((heads, rows_dev, 128), jnp.float32)
    weighted, own_sum, other_sum, lost = pl.pallas_call(
        functools.partial(match_kernel, heads, scale2, group),
        out_shape=(
            hbm_out((steps, rows, width), jnp.bfloat16),
            hbm_out((chips, size, 128), jnp.float32),
            hbm_out((chips, size, 128), jnp.float32),
            hbm_out((2 * z_size, 1, 128), jnp.float32),
        ),
        in_specs=[smem] + [vmem] * 6,
        out_specs=(hbm, hbm, hbm, pl.BlockSpec((2 * z_size, 1, 128), lambda: (0, 0, 0))),
        scratch_shapes=[pltpu.VMEM((steps, rows, width), jnp.float32)]
        + [pltpu.VMEM((steps, heads, rows_dev, 128), jnp.float32)]
        + [tile] * 4
        + [pltpu.VMEM((peers, 8, 128), jnp.float32)] * 2
        + [pltpu.VMEM((steps, rows, width), jnp.bfloat16)]
        + [pltpu.VMEM((chips, size, 128), jnp.float32)] * 2
        + [pltpu.VMEM((8, 128), jnp.float32), pltpu.SemaphoreType.DMA((heads + 2, steps))],
        compiler_params=pltpu.CompilerParams(vmem_limit_bytes=MATCH),
        cost_estimate=pl.CostEstimate(flops=6 * work * size, bytes_accessed=12 << 20, transcendentals=3 * work),
        name="match",
    )(place, own_b, other_b, q, c, c_cols, down)

    columns = [[(2 * k + c) * z_size + z for c in range(2) for z in range(z_size)] for k in range(chips)]
    lost = lax.all_to_all(lost, ("context", "head"), 0, 0, axis_index_groups=columns)

    other_sum = lax.ppermute(other_sum, "context", swap)
    sent, power = pl.pallas_call(
        scale_kernel,
        out_shape=(f32((chips, 136, 128)), f32((8, 128))),
        in_specs=[vmem] * 2,
        out_specs=(vmem,) * 2,
        compiler_params=pltpu.CompilerParams(vmem_limit_bytes=SMALL),
        name="scale",
    )(own_sum, other_sum)
    sent, lost = lax.optimization_barrier((sent.astype(jnp.float16), lost))

    extra = pl.pallas_call(
        extra_kernel,
        out_shape=f32((8, 128)),
        in_specs=[vmem] * 2,
        out_specs=vmem,
        compiler_params=pltpu.CompilerParams(vmem_limit_bytes=SMALL),
        name="extra",
    )(lost, power)

    extra = jnp.broadcast_to(extra.astype(jnp.float16), (chips, 8, 128))
    sent = lax.dynamic_update_slice(sent, extra, (0, 128, 0))
    back = lax.all_to_all(sent, "context", 0, 0, axis_index_groups=plane)
    grad_c = pl.pallas_call(
        functools.partial(grad_kernel, group),
        out_shape=f32((size, rows)),
        in_specs=[smem, vmem, vmem, hbm],
        out_specs=vmem,
        scratch_shapes=[pltpu.VMEM((steps, rows, width), jnp.bfloat16), pltpu.SemaphoreType.DMA((steps,))],
        compiler_params=pltpu.CompilerParams(vmem_limit_bytes=GRADS),
        cost_estimate=pl.CostEstimate(flops=2 * work * size, bytes_accessed=10 << 20, transcendentals=0),
        name="grads",
    )(place, own_b, other_b, pltpu.with_memory_space_constraint(weighted, hbm_out))
    grad_c = grad_c.reshape(size, heads, rows_dev).transpose(2, 1, 0)
    mine, mean = pl.pallas_call(
        functools.partial(final_kernel, heads * z_size * peers * rows_dev),
        out_shape=(f32((rows_dev, size)), f32((1, 1))),
        in_specs=[vmem],
        out_specs=(vmem, smem),
        compiler_params=pltpu.CompilerParams(vmem_limit_bytes=SMALL),
        name="final",
    )(back.astype(jnp.float32))
    return mean[0, 0], grad_c, mine[:, None, :]


def solution(mesh):
    in_specs = (
        P("context", "head", None),
        P("context", "head", None),
        P("context", "head", None),
        P("context", "head", None),
        P("context", "head"),
    )
    out_specs = (P(), P("context", "head", None), P("context", "head", None))
    return jax.shard_map(shards, mesh=mesh, in_specs=in_specs, out_specs=out_specs, check_vma=False)
```

```python
import functools
import math

import jax
import jax.numpy as jnp
from jax import lax
from jax.experimental import pallas as pl
from jax.experimental.pallas import tpu as pltpu
from jax.sharding import PartitionSpec as P

NEG = -1e30
LOG2E = math.log2(math.e)
TINY = 1e-30
FULL, SMALL, MATCH, GRADS = 60 << 20, 8 << 20, 48 << 20, 20 << 20


def dot(a, b):
    return jnp.dot(a, b, preferred_element_type=jnp.float32)


def dot_nt(a, b):
    return lax.dot_general(a, b, (((1,), (1,)), ((), ())), preferred_element_type=jnp.float32)


def pieces(x):
    high = x.astype(jnp.bfloat16)
    rest = x - high.astype(jnp.float32)
    mid = rest.astype(jnp.bfloat16)
    return high, mid, (rest - mid.astype(jnp.float32)).astype(jnp.bfloat16)


def exponent(x):
    return jnp.floor(jnp.log2(jnp.maximum(x, TINY)))


def block_kernel(keys_from, b_from, log_from, out, keys, b_rows, log_decay, block, sems):
    copies = [
        pltpu.make_async_copy(x, y, sems.at[i])
        for i, (x, y) in enumerate(((keys_from, keys), (b_from, b_rows), (log_from, log_decay)))
    ]
    for x in copies:
        x.start()
    for x in copies:
        x.wait()
    block[0:128] = keys[...].T
    block[128:256] = b_rows[...].T
    block[256:272] = jnp.concatenate(pieces(log_decay[...])[:2], axis=0)
    copies = [pltpu.make_async_copy(block, out.at[k], sems.at[3 + k]) for k in range(out.shape[0])]
    for x in copies:
        x.start()
    for x in copies:
        x.wait()


def match_kernel(heads, scale2, group, place, own_b, other_b, q_from, c_from, cols_from, log_decay,
                 weighted, own_grad, other_grad, loss, q, c, c_cols,
                 scores, tops, peak, total, fade, log_fade, key_fade, key_log, held, lost, sems, load_sems):
    chip, core = place[0], place[1]
    chips, half = own_b.shape[0], q.shape[1]
    rows = heads * half
    full = chip // group
    loads = [
        pltpu.make_async_copy(x, y, load_sems.at[i]) for i, (x, y) in enumerate(((q_from, q), (c_from, c), (cols_from, c_cols)))
    ]
    for x in loads:
        x.start()

    u = lax.broadcasted_iota(jnp.int32, (128, 128), 0)
    v = lax.broadcasted_iota(jnp.int32, (128, 128), 1)
    after = jnp.where(u > v, 1.0, 0.0).astype(jnp.bfloat16)
    upto = jnp.where(u <= v, 1.0, 0.0).astype(jnp.bfloat16)
    lower = jnp.where(u >= v, 1.0, 0.0).astype(jnp.bfloat16)
    columns = jnp.concatenate([log_decay[...], jnp.zeros((128 - heads, 128), jnp.float32)], axis=0).T
    log_rows = sum(dot(lower, part) for part in pieces(columns)[:2]) * LOG2E
    for h in range(heads):
        row_log = jnp.broadcast_to(log_rows[:, h : h + 1], (half, 128))
        log_fade[h] = row_log
        fade[h] = jnp.exp2(row_log)
    def sums(ref, matrix):
        y = dot(ref[:, 256:272].reshape(chips * 16, 128), matrix).reshape(chips, 16, 128)
        return y[:, 0:8] + y[:, 8:16]

    ones = jnp.ones((128, 128), jnp.bfloat16)
    own_tail, other_tail = sums(own_b, after), sums(other_b, after)
    own_sum, other_sum = sums(own_b, ones), sums(other_b, ones)
    own_head = sums(own_b, upto)
    behind = jnp.zeros((8, 128), jnp.float32)
    for k in range(chips - 1, -1, -1):
        own = own_tail[k] + behind + jnp.where(core == 0, other_sum[k], 0.0)
        own = jnp.where(chip > k, own, -own_head[k]) * LOG2E
        other = behind + jnp.where(core == 0, 0.0, own_sum[k])
        other = (other_tail[k] + jnp.where(chip > k, other, 0.0)) * LOG2E
        for side, logs in enumerate((own, other)):
            key_log[2 * k + side] = logs
            key_fade[2 * k + side] = jnp.exp2(jnp.minimum(logs, 0.0))
        here = jnp.where(core == 0, 0.0, other_sum[k])
        behind = behind + jnp.where(chip > k, own_sum[k] + other_sum[k], jnp.where(chip == k, here, 0.0))

    def wide(x):
        return jnp.concatenate([x] * (2 * group), axis=1)

    def of_group(p, first):
        return jnp.concatenate(
            [ref[group * p + i, first : first + 128] for i in range(group) for ref in (own_b, other_b)], axis=1
        )

    def causal(p):
        apart = [2 * (group * p + i - chip) + side * (1 - 2 * core) for i in range(group) for side in range(2)]
        return jnp.concatenate([u - v >= 128 * x for x in apart], axis=1)

    peak[...] = jnp.full_like(peak, NEG)
    total[...] = jnp.zeros_like(total)

    def score(p, masked):
        s = dot(q[...].reshape(rows, 128), of_group(p, 0)) * scale2
        seen = causal(p) if masked else None
        for h in range(heads):
            at = slice(h * half, h * half + half)
            x = s[at]
            if masked:
                x = jnp.where(seen, x, NEG)
            parts = [x[:, 128 * i : 128 * i + 128] for i in range(2 * group)]
            old = peak[h]
            top = functools.reduce(jnp.maximum, parts, old)
            grown = [jnp.exp2(y - top) for y in parts]
            for i in range(2 * group):
                scores[p, at, 128 * i : 128 * i + 128] = grown[i]
            total[h] = total[h] * jnp.exp2(old - top) + sum(grown)
            peak[h] = top
            tops[p, h] = top

    loads[0].wait()

    @pl.loop(0, full)
    def _(p):
        score(p, False)

    score(full, True)

    for h in range(heads):
        top = jnp.max(peak[h], axis=1, keepdims=True)
        summed = jnp.sum(total[h] * jnp.exp2(peak[h] - top), axis=1, keepdims=True)
        peak[h] = jnp.broadcast_to(top + jnp.log2(summed), (half, 128))
    lost[...] = jnp.zeros_like(lost)

    def copy(p, h):
        at = pl.ds(h * half, half)
        return pltpu.make_async_copy(held.at[p, at], weighted.at[p, at], sems.at[h, p])

    @pl.loop(full + 1, chips // group)
    def _(p):
        for i in range(group):
            own_grad[group * p + i] = jnp.zeros((128, 128), jnp.float32)
            other_grad[group * p + i] = jnp.zeros((128, 128), jnp.float32)

    def step(p, masked):
        kept = [2 * group * p + i for i in range(2 * group)]
        inner = dot(c[...].reshape(rows, 128), of_group(p, 128))
        seen = causal(p) if masked else None
        squares = jnp.zeros((8, 128), jnp.float32)
        for h in range(heads):
            at = slice(h * half, h * half + half)
            teacher = scores[p, at] * wide(jnp.exp2(tops[p, h] - peak[h]))
            if masked:
                logs = wide(log_fade[h]) + jnp.concatenate([key_log[k, h : h + 1] for k in kept], axis=1)
                decay = jnp.exp2(jnp.where(seen, logs, NEG))
            else:
                decay = wide(fade[h]) * jnp.concatenate([key_fade[k, h : h + 1] for k in kept], axis=1)
            mismatch = inner[at] * decay - teacher
            square = jnp.sum((mismatch * mismatch).reshape(half // 8, 8, 256 * group), axis=0)
            for i in range(2 * group):
                squares = squares + square[:, 128 * i : 128 * i + 128]
            held[p, at] = (mismatch * decay).astype(jnp.bfloat16)
            copy(p, h).start()
        lost[...] += squares
        parts = dot(c_cols[...], held[p])
        for i in range(group):
            own_grad[group * p + i] = parts[:, 256 * i : 256 * i + 128]
            other_grad[group * p + i] = parts[:, 256 * i + 128 : 256 * i + 256]

    loads[1].wait()
    loads[2].wait()

    @pl.loop(0, full)
    def _(p):
        step(p, False)

    step(full, True)
    loss[...] = jnp.broadcast_to(jnp.sum(lost[...], keepdims=True)[None], loss.shape)

    @pl.loop(0, full + 1)
    def _(p):
        for h in range(heads):
            copy(p, h).wait()


def grad_kernel(group, place, own_b, other_b, weighted, grad_c, held, sems):
    full = place[0] // group

    def copy(p):
        return pltpu.make_async_copy(weighted.at[p], held.at[p], sems.at[p])

    @pl.loop(0, full + 1)
    def _(p):
        copy(p).start()

    grad_c[...] = jnp.zeros_like(grad_c)

    @pl.loop(0, full + 1)
    def _(p):
        copy(p).wait()
        b_cols = jnp.concatenate(
            [ref[group * p + i, 128:256] for i in range(group) for ref in (own_b, other_b)], axis=1
        )
        grad_c[...] += 2.0 * dot_nt(b_cols, held[p])


def scale_kernel(own, other, sent, power):
    blocks = own.shape[0]
    top = jnp.zeros((128, 128), jnp.float32)
    for k in range(blocks):
        x = own[k] + other[k]
        sent[k, 0:128] = x
        top = jnp.maximum(top, jnp.abs(x))
    level = exponent(jnp.broadcast_to(jnp.max(top, keepdims=True), (128, 128)))
    up = jnp.exp2(13.0 - level)
    for k in range(blocks):
        sent[k, 0:128] = sent[k, 0:128] * up
        sent[k, 128:136] = jnp.zeros((8, 128), jnp.float32)
    power[...] = level[0:8]


def extra_kernel(lost, power, extra):
    total = jnp.broadcast_to(jnp.sum(lost[...], axis=0), (8, 128))
    lost_power = exponent(total)
    share = total * jnp.exp2(-lost_power)
    coarse = jnp.floor(share * 1024.0) * (1.0 / 1024.0)
    lane = lax.broadcasted_iota(jnp.int32, (8, 128), 1)
    row = jnp.where(lane == 0, power[...], 0.0)
    row = jnp.where(lane == 1, lost_power, row)
    row = jnp.where(lane == 2, coarse, row)
    row = jnp.where(lane == 3, (share - coarse) * 1024.0, row)
    extra[...] = row


def final_kernel(count, back, grad_b, mean):
    blocks = back.shape[0]
    total = jnp.zeros((128, 128), jnp.float32)
    loss = jnp.zeros((1, 128), jnp.float32)
    for k in range(blocks):
        extra = back[k, 128:129]
        power = jnp.broadcast_to(extra[:, 0:1], (1, 128))
        total = total + back[k, 0:128] * jnp.exp2(power - 13.0)
        share = extra[:, 2:3] + extra[:, 3:4] * (1.0 / 1024.0)
        loss = loss + jnp.broadcast_to(share * jnp.exp2(extra[:, 1:2]), (1, 128))
    grad_b[...] = 2.0 * total.T
    mean[0, 0] = jnp.max(loss) * (1.0 / count)


def shards(queries, keys, c_proj, b_proj, log_decay):
    rows_dev, heads, size = queries.shape
    peers = lax.axis_size("context")
    z_size = lax.axis_size("head")
    chips = peers // 2
    rows = heads * rows_dev
    group = 4
    here = lax.axis_index("context")
    place = jnp.stack([here // 2, here % 2]).astype(jnp.int32)
    scale2 = LOG2E / math.sqrt(size)
    plane = [[2 * k + c for k in range(chips)] for c in range(2)]
    swap = [(i, i ^ 1) for i in range(peers)]

    f32 = functools.partial(jax.ShapeDtypeStruct, dtype=jnp.float32)
    bf16 = functools.partial(jax.ShapeDtypeStruct, dtype=jnp.bfloat16)
    smem = pl.BlockSpec(memory_space=pltpu.SMEM)
    vmem = pl.BlockSpec(memory_space=pltpu.VMEM)
    hbm_out = pltpu.MemorySpace.HBM
    hbm = pl.BlockSpec(memory_space=hbm_out)
    work = rows * peers * 128
    steps = chips // group
    width = 256 * group

    down = log_decay.T
    block = pl.pallas_call(
        block_kernel,
        out_shape=hbm_out((chips, 272, 128), jnp.bfloat16),
        in_specs=[hbm] * 3,
        out_specs=hbm,
        scratch_shapes=[pltpu.VMEM((rows_dev, size), jnp.bfloat16)] * 2
        + [pltpu.VMEM((heads, rows_dev), jnp.float32), pltpu.VMEM((272, 128), jnp.bfloat16)]
        + [pltpu.SemaphoreType.DMA((3 + chips,))],
        compiler_params=pltpu.CompilerParams(vmem_limit_bytes=SMALL),
        name="block",
    )(*(pltpu.with_memory_space_constraint(x, hbm_out) for x in (keys[:, 0], b_proj[:, 0], down)))
    own_b = lax.all_to_all(block, "context", 0, 0, axis_index_groups=plane)
    q, c = queries.transpose(1, 0, 2), c_proj.transpose(1, 0, 2)
    c_cols = c_proj.transpose(2, 1, 0).reshape(size, rows)
    own_b, q, c, c_cols, place = lax.optimization_barrier((own_b, q, c, c_cols, place))
    other_b = lax.ppermute(own_b, "context", swap)
    tile = pltpu.VMEM((heads, rows_dev, 128), jnp.float32)
    weighted, own_sum, other_sum, lost = pl.pallas_call(
        functools.partial(match_kernel, heads, scale2, group),
        out_shape=(
            hbm_out((steps, rows, width), jnp.bfloat16),
            f32((chips, size, 128)),
            f32((chips, size, 128)),
            hbm_out((2 * z_size, 1, 128), jnp.float32),
        ),
        in_specs=[smem, vmem, vmem, hbm, hbm, hbm, vmem],
        out_specs=(hbm, vmem, vmem, pl.BlockSpec((2 * z_size, 1, 128), lambda: (0, 0, 0))),
        scratch_shapes=[pltpu.VMEM((heads, rows_dev, size), jnp.bfloat16)] * 2
        + [pltpu.VMEM((size, rows), jnp.bfloat16), pltpu.VMEM((steps, rows, width), jnp.float32)]
        + [pltpu.VMEM((steps, heads, rows_dev, 128), jnp.float32)]
        + [tile] * 4
        + [pltpu.VMEM((peers, 8, 128), jnp.float32)] * 2
        + [pltpu.VMEM((steps, rows, width), jnp.bfloat16)]
        + [pltpu.VMEM((8, 128), jnp.float32), pltpu.SemaphoreType.DMA((heads, steps)), pltpu.SemaphoreType.DMA((3,))],
        compiler_params=pltpu.CompilerParams(vmem_limit_bytes=MATCH),
        cost_estimate=pl.CostEstimate(flops=6 * work * size, bytes_accessed=12 << 20, transcendentals=3 * work),
        name="match",
    )(place, own_b, other_b, *(pltpu.with_memory_space_constraint(x, hbm_out) for x in (q, c, c_cols)), down)

    columns = [[(2 * k + c) * z_size + z for c in range(2) for z in range(z_size)] for k in range(chips)]
    lost = lax.all_to_all(lost, ("context", "head"), 0, 0, axis_index_groups=columns)

    other_sum = lax.ppermute(other_sum, "context", swap)
    sent, power = pl.pallas_call(
        scale_kernel,
        out_shape=(f32((chips, 136, 128)), f32((8, 128))),
        in_specs=[vmem] * 2,
        out_specs=(vmem,) * 2,
        compiler_params=pltpu.CompilerParams(vmem_limit_bytes=SMALL),
        name="scale",
    )(own_sum, other_sum)
    sent, lost = lax.optimization_barrier((sent.astype(jnp.float16), lost))

    extra = pl.pallas_call(
        extra_kernel,
        out_shape=f32((8, 128)),
        in_specs=[vmem] * 2,
        out_specs=vmem,
        compiler_params=pltpu.CompilerParams(vmem_limit_bytes=SMALL),
        name="extra",
    )(lost, power)

    extra = jnp.broadcast_to(extra.astype(jnp.float16), (chips, 8, 128))
    sent = lax.dynamic_update_slice(sent, extra, (0, 128, 0))
    back = lax.all_to_all(sent, "context", 0, 0, axis_index_groups=plane)
    grad_c = pl.pallas_call(
        functools.partial(grad_kernel, group),
        out_shape=f32((size, rows)),
        in_specs=[smem, vmem, vmem, hbm],
        out_specs=vmem,
        scratch_shapes=[pltpu.VMEM((steps, rows, width), jnp.bfloat16), pltpu.SemaphoreType.DMA((steps,))],
        compiler_params=pltpu.CompilerParams(vmem_limit_bytes=GRADS),
        cost_estimate=pl.CostEstimate(flops=2 * work * size, bytes_accessed=10 << 20, transcendentals=0),
        name="grads",
    )(place, own_b, other_b, pltpu.with_memory_space_constraint(weighted, hbm_out))
    grad_c = grad_c.reshape(size, heads, rows_dev).transpose(2, 1, 0)
    mine, mean = pl.pallas_call(
        functools.partial(final_kernel, heads * z_size * peers * rows_dev),
        out_shape=(f32((rows_dev, size)), f32((1, 1))),
        in_specs=[vmem],
        out_specs=(vmem, smem),
        compiler_params=pltpu.CompilerParams(vmem_limit_bytes=SMALL),
        name="final",
    )(back.astype(jnp.float32))
    return mean[0, 0], grad_c, mine[:, None, :]


def solution(mesh):
    in_specs = (
        P("context", "head", None),
        P("context", "head", None),
        P("context", "head", None),
        P("context", "head", None),
        P("context", "head"),
    )
    out_specs = (P(), P("context", "head", None), P("context", "head", None))
    return jax.shard_map(shards, mesh=mesh, in_specs=in_specs, out_specs=out_specs, check_vma=False)
```

```python
import functools
import math

import jax
import jax.numpy as jnp
from jax import lax
from jax.experimental import pallas as pl
from jax.experimental.pallas import tpu as pltpu
from jax.sharding import PartitionSpec as P

NEG = -1e30
LOG2E = math.log2(math.e)
TINY = 1e-30
FULL, SMALL, MATCH, GRADS = 60 << 20, 8 << 20, 48 << 20, 20 << 20


def dot(a, b):
    return jnp.dot(a, b, preferred_element_type=jnp.float32)


def dot_nt(a, b):
    return lax.dot_general(a, b, (((1,), (1,)), ((), ())), preferred_element_type=jnp.float32)


def pieces(x):
    high = x.astype(jnp.bfloat16)
    rest = x - high.astype(jnp.float32)
    mid = rest.astype(jnp.bfloat16)
    return high, mid, (rest - mid.astype(jnp.float32)).astype(jnp.bfloat16)


def exponent(x):
    return jnp.floor(jnp.log2(jnp.maximum(x, TINY)))


def block_kernel(keys_from, b_from, log_from, out, keys, b_rows, log_decay, block, sems):
    copies = [
        pltpu.make_async_copy(x, y, sems.at[i])
        for i, (x, y) in enumerate(((keys_from, keys), (b_from, b_rows), (log_from, log_decay)))
    ]
    for x in copies:
        x.start()
    for x in copies:
        x.wait()
    block[0:128] = keys[...].T
    block[128:256] = b_rows[...].T
    block[256:272] = jnp.concatenate(pieces(log_decay[...])[:2], axis=0)
    copies = [pltpu.make_async_copy(block, out.at[k], sems.at[3 + k]) for k in range(out.shape[0])]
    for x in copies:
        x.start()
    for x in copies:
        x.wait()


def match_kernel(heads, scale2, group, place, own_b, other_b, q, c, c_cols, log_decay, weighted, own_grad, other_grad, loss,
                 scores, tops, peak, total, fade, log_fade, key_fade, key_log, held, own_held, other_held, lost, sems):
    chip, core = place[0], place[1]
    chips, half = own_b.shape[0], q.shape[1]
    rows = heads * half
    full = chip // group

    u = lax.broadcasted_iota(jnp.int32, (128, 128), 0)
    v = lax.broadcasted_iota(jnp.int32, (128, 128), 1)
    after = jnp.where(u > v, 1.0, 0.0).astype(jnp.bfloat16)
    upto = jnp.where(u <= v, 1.0, 0.0).astype(jnp.bfloat16)
    lower = jnp.where(u >= v, 1.0, 0.0).astype(jnp.bfloat16)
    columns = jnp.concatenate([log_decay[...], jnp.zeros((128 - heads, 128), jnp.float32)], axis=0).T
    log_rows = sum(dot(lower, part) for part in pieces(columns)[:2]) * LOG2E
    for h in range(heads):
        row_log = jnp.broadcast_to(log_rows[:, h : h + 1], (half, 128))
        log_fade[h] = row_log
        fade[h] = jnp.exp2(row_log)
    def sums(ref, matrix):
        y = dot(ref[:, 256:272].reshape(chips * 16, 128), matrix).reshape(chips, 16, 128)
        return y[:, 0:8] + y[:, 8:16]

    ones = jnp.ones((128, 128), jnp.bfloat16)
    own_tail, other_tail = sums(own_b, after), sums(other_b, after)
    own_sum, other_sum = sums(own_b, ones), sums(other_b, ones)
    own_head = sums(own_b, upto)
    behind = jnp.zeros((8, 128), jnp.float32)
    for k in range(chips - 1, -1, -1):
        own = own_tail[k] + behind + jnp.where(core == 0, other_sum[k], 0.0)
        own = jnp.where(chip > k, own, -own_head[k]) * LOG2E
        other = behind + jnp.where(core == 0, 0.0, own_sum[k])
        other = (other_tail[k] + jnp.where(chip > k, other, 0.0)) * LOG2E
        for side, logs in enumerate((own, other)):
            key_log[2 * k + side] = logs
            key_fade[2 * k + side] = jnp.exp2(jnp.minimum(logs, 0.0))
        here = jnp.where(core == 0, 0.0, other_sum[k])
        behind = behind + jnp.where(chip > k, own_sum[k] + other_sum[k], jnp.where(chip == k, here, 0.0))

    def wide(x):
        return jnp.concatenate([x] * (2 * group), axis=1)

    def of_group(p, first):
        return jnp.concatenate(
            [ref[group * p + i, first : first + 128] for i in range(group) for ref in (own_b, other_b)], axis=1
        )

    def causal(p):
        apart = [2 * (group * p + i - chip) + side * (1 - 2 * core) for i in range(group) for side in range(2)]
        return jnp.concatenate([u - v >= 128 * x for x in apart], axis=1)

    peak[...] = jnp.full_like(peak, NEG)
    total[...] = jnp.zeros_like(total)

    def score(p, masked):
        s = dot(q[...].reshape(rows, 128), of_group(p, 0)) * scale2
        seen = causal(p) if masked else None
        for h in range(heads):
            at = slice(h * half, h * half + half)
            x = s[at]
            if masked:
                x = jnp.where(seen, x, NEG)
            parts = [x[:, 128 * i : 128 * i + 128] for i in range(2 * group)]
            old = peak[h]
            top = functools.reduce(jnp.maximum, parts, old)
            grown = [jnp.exp2(y - top) for y in parts]
            for i in range(2 * group):
                scores[p, at, 128 * i : 128 * i + 128] = grown[i]
            total[h] = total[h] * jnp.exp2(old - top) + sum(grown)
            peak[h] = top
            tops[p, h] = top

    @pl.loop(0, full)
    def _(p):
        score(p, False)

    score(full, True)

    for h in range(heads):
        top = jnp.max(peak[h], axis=1, keepdims=True)
        summed = jnp.sum(total[h] * jnp.exp2(peak[h] - top), axis=1, keepdims=True)
        peak[h] = jnp.broadcast_to(top + jnp.log2(summed), (half, 128))
    lost[...] = jnp.zeros_like(lost)

    def copies(p):
        part = pl.ds(p * group, group)
        return (
            pltpu.make_async_copy(own_held.at[part], own_grad.at[part], sems.at[heads, p]),
            pltpu.make_async_copy(other_held.at[part], other_grad.at[part], sems.at[heads + 1, p]),
        )

    def copy(p, h):
        at = pl.ds(h * half, half)
        return pltpu.make_async_copy(held.at[p, at], weighted.at[p, at], sems.at[h, p])

    @pl.loop(full + 1, chips // group)
    def _(p):
        for i in range(group):
            own_held[group * p + i] = jnp.zeros((128, 128), jnp.float32)
            other_held[group * p + i] = jnp.zeros((128, 128), jnp.float32)
        for x in copies(p):
            x.start()

    def step(p, masked):
        kept = [2 * group * p + i for i in range(2 * group)]
        inner = dot(c[...].reshape(rows, 128), of_group(p, 128))
        seen = causal(p) if masked else None
        squares = jnp.zeros((8, 128), jnp.float32)
        for h in range(heads):
            at = slice(h * half, h * half + half)
            teacher = scores[p, at] * wide(jnp.exp2(tops[p, h] - peak[h]))
            if masked:
                logs = wide(log_fade[h]) + jnp.concatenate([key_log[k, h : h + 1] for k in kept], axis=1)
                decay = jnp.exp2(jnp.where(seen, logs, NEG))
            else:
                decay = wide(fade[h]) * jnp.concatenate([key_fade[k, h : h + 1] for k in kept], axis=1)
            mismatch = inner[at] * decay - teacher
            square = jnp.sum((mismatch * mismatch).reshape(half // 8, 8, 256 * group), axis=0)
            for i in range(2 * group):
                squares = squares + square[:, 128 * i : 128 * i + 128]
            held[p, at] = (mismatch * decay).astype(jnp.bfloat16)
            copy(p, h).start()
        lost[...] += squares
        parts = dot(c_cols[...], held[p])
        for i in range(group):
            own_held[group * p + i] = parts[:, 256 * i : 256 * i + 128]
            other_held[group * p + i] = parts[:, 256 * i + 128 : 256 * i + 256]
        for x in copies(p):
            x.start()

    @pl.when(full == chips // group - 1)
    def _():
        for p in range(chips // group - 1):
            step(p, False)
        step(chips // group - 1, True)

    @pl.when(full < chips // group - 1)
    def _():
        @pl.loop(0, full)
        def _(p):
            step(p, False)

        step(full, True)
    loss[...] = jnp.broadcast_to(jnp.sum(lost[...], keepdims=True)[None], loss.shape)

    @pl.loop(0, full + 1)
    def _(p):
        for h in range(heads):
            copy(p, h).wait()

    @pl.loop(0, chips // group)
    def _(p):
        for x in copies(p):
            x.wait()


def grad_kernel(group, place, own_b, other_b, weighted, grad_c, held, sems):
    full = place[0] // group

    def copy(p):
        return pltpu.make_async_copy(weighted.at[p], held.at[p], sems.at[p])

    @pl.loop(0, full + 1)
    def _(p):
        copy(p).start()

    grad_c[...] = jnp.zeros_like(grad_c)

    @pl.loop(0, full + 1)
    def _(p):
        copy(p).wait()
        b_cols = jnp.concatenate(
            [ref[group * p + i, 128:256] for i in range(group) for ref in (own_b, other_b)], axis=1
        )
        grad_c[...] += 2.0 * dot_nt(b_cols, held[p])


def scale_kernel(own, other, sent, power):
    blocks = own.shape[0]
    top = jnp.zeros((128, 128), jnp.float32)
    for k in range(blocks):
        x = own[k] + other[k]
        sent[k, 0:128] = x
        top = jnp.maximum(top, jnp.abs(x))
    level = exponent(jnp.broadcast_to(jnp.max(top, keepdims=True), (128, 128)))
    up = jnp.exp2(13.0 - level)
    for k in range(blocks):
        sent[k, 0:128] = sent[k, 0:128] * up
        sent[k, 128:136] = jnp.zeros((8, 128), jnp.float32)
    power[...] = level[0:8]


def extra_kernel(lost, power, extra):
    total = jnp.broadcast_to(jnp.sum(lost[...], axis=0), (8, 128))
    lost_power = exponent(total)
    share = total * jnp.exp2(-lost_power)
    coarse = jnp.floor(share * 1024.0) * (1.0 / 1024.0)
    lane = lax.broadcasted_iota(jnp.int32, (8, 128), 1)
    row = jnp.where(lane == 0, power[...], 0.0)
    row = jnp.where(lane == 1, lost_power, row)
    row = jnp.where(lane == 2, coarse, row)
    row = jnp.where(lane == 3, (share - coarse) * 1024.0, row)
    extra[...] = row


def final_kernel(count, back, grad_b, mean):
    blocks = back.shape[0]
    extra = jnp.concatenate([back[k, 128:129] for k in range(blocks)], axis=0)
    scale = jnp.broadcast_to(jnp.exp2(extra[:, 0:1] - 13.0), (blocks, 128))
    total = jnp.zeros((128, 128), jnp.float32)
    for k in range(blocks):
        total = total + back[k, 0:128] * scale[k : k + 1]
    grad_b[...] = 2.0 * total.T
    share = extra[:, 2:3] + extra[:, 3:4] * (1.0 / 1024.0)
    mean[0, 0] = jnp.sum(share * jnp.exp2(extra[:, 1:2])) * (1.0 / count)


def shards(queries, keys, c_proj, b_proj, log_decay):
    rows_dev, heads, size = queries.shape
    peers = lax.axis_size("context")
    z_size = lax.axis_size("head")
    chips = peers // 2
    rows = heads * rows_dev
    group = 4
    here = lax.axis_index("context")
    place = jnp.stack([here // 2, here % 2]).astype(jnp.int32)
    scale2 = LOG2E / math.sqrt(size)
    plane = [[2 * k + c for k in range(chips)] for c in range(2)]
    swap = [(i, i ^ 1) for i in range(peers)]

    f32 = functools.partial(jax.ShapeDtypeStruct, dtype=jnp.float32)
    bf16 = functools.partial(jax.ShapeDtypeStruct, dtype=jnp.bfloat16)
    smem = pl.BlockSpec(memory_space=pltpu.SMEM)
    vmem = pl.BlockSpec(memory_space=pltpu.VMEM)
    hbm_out = pltpu.MemorySpace.HBM
    hbm = pl.BlockSpec(memory_space=hbm_out)
    work = rows * peers * 128
    steps = chips // group
    width = 256 * group

    down = log_decay.T
    block = pl.pallas_call(
        block_kernel,
        out_shape=hbm_out((chips, 272, 128), jnp.bfloat16),
        in_specs=[hbm] * 3,
        out_specs=hbm,
        scratch_shapes=[pltpu.VMEM((rows_dev, size), jnp.bfloat16)] * 2
        + [pltpu.VMEM((heads, rows_dev), jnp.float32), pltpu.VMEM((272, 128), jnp.bfloat16)]
        + [pltpu.SemaphoreType.DMA((3 + chips,))],
        compiler_params=pltpu.CompilerParams(vmem_limit_bytes=SMALL),
        name="block",
    )(*(pltpu.with_memory_space_constraint(x, hbm_out) for x in (keys[:, 0], b_proj[:, 0], down)))
    own_b = lax.all_to_all(block, "context", 0, 0, axis_index_groups=plane)
    q, c = queries.transpose(1, 0, 2), c_proj.transpose(1, 0, 2)
    c_cols = c_proj.transpose(2, 1, 0).reshape(size, rows)
    own_b, q, c, c_cols, place = lax.optimization_barrier((own_b, q, c, c_cols, place))
    other_b = lax.ppermute(own_b, "context", swap)
    tile = pltpu.VMEM((heads, rows_dev, 128), jnp.float32)
    weighted, own_sum, other_sum, lost = pl.pallas_call(
        functools.partial(match_kernel, heads, scale2, group),
        out_shape=(
            hbm_out((steps, rows, width), jnp.bfloat16),
            hbm_out((chips, size, 128), jnp.float32),
            hbm_out((chips, size, 128), jnp.float32),
            hbm_out((2 * z_size, 1, 128), jnp.float32),
        ),
        in_specs=[smem] + [vmem] * 6,
        out_specs=(hbm, hbm, hbm, pl.BlockSpec((2 * z_size, 1, 128), lambda: (0, 0, 0))),
        scratch_shapes=[pltpu.VMEM((steps, rows, width), jnp.float32)]
        + [pltpu.VMEM((steps, heads, rows_dev, 128), jnp.float32)]
        + [tile] * 4
        + [pltpu.VMEM((peers, 8, 128), jnp.float32)] * 2
        + [pltpu.VMEM((steps, rows, width), jnp.bfloat16)]
        + [pltpu.VMEM((chips, size, 128), jnp.float32)] * 2
        + [pltpu.VMEM((8, 128), jnp.float32), pltpu.SemaphoreType.DMA((heads + 2, steps))],
        compiler_params=pltpu.CompilerParams(vmem_limit_bytes=MATCH),
        cost_estimate=pl.CostEstimate(flops=6 * work * size, bytes_accessed=12 << 20, transcendentals=3 * work),
        name="match",
    )(place, own_b, other_b, q, c, c_cols, down)

    columns = [[(2 * k + c) * z_size + z for c in range(2) for z in range(z_size)] for k in range(chips)]
    lost = lax.all_to_all(lost, ("context", "head"), 0, 0, axis_index_groups=columns)

    other_sum = lax.ppermute(other_sum, "context", swap)
    sent, power = pl.pallas_call(
        scale_kernel,
        out_shape=(f32((chips, 136, 128)), f32((8, 128))),
        in_specs=[vmem] * 2,
        out_specs=(vmem,) * 2,
        compiler_params=pltpu.CompilerParams(vmem_limit_bytes=SMALL),
        name="scale",
    )(own_sum, other_sum)
    sent, lost = lax.optimization_barrier((sent.astype(jnp.float16), lost))

    extra = pl.pallas_call(
        extra_kernel,
        out_shape=f32((8, 128)),
        in_specs=[vmem] * 2,
        out_specs=vmem,
        compiler_params=pltpu.CompilerParams(vmem_limit_bytes=SMALL),
        name="extra",
    )(lost, power)

    extra = jnp.broadcast_to(extra.astype(jnp.float16), (chips, 8, 128))
    sent = lax.dynamic_update_slice(sent, extra, (0, 128, 0))
    back = lax.all_to_all(sent, "context", 0, 0, axis_index_groups=plane)
    grad_c = pl.pallas_call(
        functools.partial(grad_kernel, group),
        out_shape=f32((size, rows)),
        in_specs=[smem, vmem, vmem, hbm],
        out_specs=vmem,
        scratch_shapes=[pltpu.VMEM((steps, rows, width), jnp.bfloat16), pltpu.SemaphoreType.DMA((steps,))],
        compiler_params=pltpu.CompilerParams(vmem_limit_bytes=GRADS),
        cost_estimate=pl.CostEstimate(flops=2 * work * size, bytes_accessed=10 << 20, transcendentals=0),
        name="grads",
    )(place, own_b, other_b, pltpu.with_memory_space_constraint(weighted, hbm_out))
    grad_c = grad_c.reshape(size, heads, rows_dev).transpose(2, 1, 0)
    mine, mean = pl.pallas_call(
        functools.partial(final_kernel, heads * z_size * peers * rows_dev),
        out_shape=(f32((rows_dev, size)), f32((1, 1))),
        in_specs=[vmem],
        out_specs=(vmem, smem),
        compiler_params=pltpu.CompilerParams(vmem_limit_bytes=SMALL),
        name="final",
    )(back.astype(jnp.float32))
    return mean[0, 0], grad_c, mine[:, None, :]


def solution(mesh):
    in_specs = (
        P("context", "head", None),
        P("context", "head", None),
        P("context", "head", None),
        P("context", "head", None),
        P("context", "head"),
    )
    out_specs = (P(), P("context", "head", None), P("context", "head", None))
    return jax.shard_map(shards, mesh=mesh, in_specs=in_specs, out_specs=out_specs, check_vma=False)
```
